256 devices in a mesh: dp: 2 (over z_hi), space: 128 (over y, x, z_lo, core).
Axes of the slice: x: 4, y: 4, z: 8 (z_hi: 2, z_lo: 4; z = z_hi * 4 + z_lo), core: 2. Of those that a mesh axis runs over, the one named last changes fastest.
Arguments:
- fields: bfloat16 [2, 256, 16, 16, 128], P('dp', 'space'), may hold values from -6 to 6
- cotangent: bfloat16 [2, 256, 16, 16, 128], P('dp', 'space'), may hold values from -6 to 6
- ocean_mask: int32 [256, 16, 16], P('space'), may hold values from 0 to 1, as said below
- neighbors: int32 [256, 8], P('space'), may hold values from -1 to 255, as said below
- codes: int32 [256, 8], P('space'), may hold values from 0 to 3, as said below
- dw_kernel: float32 [2, 49, 128], replicated, may hold values from -0.875 to 0.875
- dw_bias: float32 [2, 128], replicated, may hold values from -3 to 3
- ln_gain: float32 [2, 128], replicated, may hold values from 0.5 to 1.5
- ln_bias: float32 [2, 128], replicated, may hold values from -3 to 3
- w_in: bfloat16 [2, 128, 512], replicated, may hold values from -0.5 to 0.5
- b_in: float32 [2, 512], replicated, may hold values from -3 to 3
- w_out: bfloat16 [2, 512, 128], replicated, may hold values from -0.25 to 0.25
- b_out: float32 [2, 128], replicated, may hold values from -2 to 2
Outputs:
- out_fields: bfloat16 [2, 256, 16, 16, 128], P('dp', 'space')
- field_grad: bfloat16 [2, 256, 16, 16, 128], P('dp', 'space')
- g_dw_kernel: float32 [2, 49, 128], replicated
- g_dw_bias: float32 [2, 128], replicated
- g_ln_gain: float32 [2, 128], replicated
- g_ln_bias: float32 [2, 128], replicated
- g_w_in: float32 [2, 128, 512], replicated
- g_b_in: float32 [2, 512], replicated
- g_w_out: float32 [2, 512, 128], replicated
- g_b_out: float32 [2, 128], replicated
The draws below stay inside these ranges and needn't reach their ends.
Inputs may be any that keep to these rules, and one draw needn't show every extreme that they name: neighbors[t, q] for q = 0..3 is the tile beside side q of tile t (0 rows 0..2, 1 the last columns, 2 the last rows, 3 columns 0..2) and for q = 4..7 the tile at corner q - 4 (first row and column, first row and last column, last row and last column, last row and first column), or -1 where there is none. Tile t lies on device t // 2 of space; every listed tile lies on a device whose space index differs from that of t by at most 2 counted around the axis, and differences of 2 in both directions occur. A listed tile always has ocean cells; a tile without ocean cells lists none. codes[t, q] names which side (q < 4) or corner (q >= 4) of the listed tile touches tile t, in the same numbering. `ocean_mask`: every device holds between 1 and 2 tiles with ocean cells; the first and the last device of space hold 2.
All inputs are finite; a program needn't handle non-finite values.
Results may differ from the reference program's by a relative error of at most 0.0095.
Values may be sent and summed in bfloat16 or wider, within the bound.
No kernel may reach another device: no remote copies, remote signals or barrier semaphores. Data moves between devices by JAX's collectives and lax.ppermute only.
A program may use at most 64 MiB of HBM per device.

```python
import math
import jax
import jax.numpy as jnp
from jax import lax

C = 128
F = 512
TS = 16
SLOTS = 2
RANGE = 2
BLOCKS = 2
BATCH = 2
TILES = 256
CELLS = 131072


def tile_graph(key):
    devices = TILES // SLOTS
    tile_ids = jnp.arange(TILES, dtype=jnp.int32)
    home_dev = tile_ids // SLOTS
    slot_of = tile_ids % SLOTS
    living = (slot_of == 0) | (jax.random.randint(jax.random.fold_in(key, 11), (TILES,), 0, 10) < 7)
    living = living | (home_dev == 0) | (home_dev == devices - 1)
    offsets = jax.random.randint(jax.random.fold_in(key, 12), (TILES, 8), -RANGE, RANGE + 1)
    offsets = offsets.at[0, 0].set(RANGE).at[0, 2].set(-RANGE).at[0, 1].set(-1)
    chosen = jax.random.randint(jax.random.fold_in(key, 13), (TILES, 8), 0, SLOTS)
    chosen = chosen.at[0, 1].set(SLOTS - 1)
    owner_dev = (home_dev[:, None] + offsets) % devices
    target = owner_dev * SLOTS + chosen
    target = jnp.where(living[target], target, owner_dev * SLOTS)
    absent = jax.random.randint(jax.random.fold_in(key, 14), (TILES, 8), 0, 8) == 0
    absent = absent.at[0, 0:3].set(False)
    linked = jnp.where(absent | jnp.logical_not(living)[:, None], -1, target)
    turn_codes = jax.random.randint(jax.random.fold_in(key, 15), (TILES, 8), 0, 4)
    return (living, linked.astype(jnp.int32), turn_codes.astype(jnp.int32))


def draw_ocean_mask(key, part):
    living = tile_graph(key)[0]
    wet_cells = jax.random.randint(jax.random.fold_in(key, 16), (TILES, TS, TS), 0, 4) < 3
    return (wet_cells & living[:, None, None]).astype(jnp.int32)


def draw_neighbors(key, part):
    return tile_graph(key)[1]


def draw_codes(key, part):
    return tile_graph(key)[2]


def shard_levels(stream_key, extent, shards, least, high):
    def one(axis_at, parts):
        draws = jax.random.uniform(jax.random.fold_in(jax.random.fold_in(stream_key, 6), axis_at), (parts,), jnp.float32, least / len(shards), high / len(shards))
        return jnp.repeat(jnp.exp(draws), extent[axis_at] // parts).reshape((-1,) + (1,) * (len(extent) - axis_at - 1))

    factor_of = one(*shards[0])
    for cut in shards[1:]:
        factor_of = factor_of * one(*cut)
    return factor_of


def scatter_about(key, extent, spread, reach, split=(), kind=jnp.bfloat16):
    array = jax.random.normal(key, extent, jnp.float32) * spread
    if len(split) > 0:
        array = shard_levels(key, extent, split, -0.22, 0.18) * array
    return jnp.clip(array, min=-reach, max=reach).astype(kind)


def setup_inputs(seed: int = 0) -> dict:
    key_list = jax.random.split(jax.random.key(seed), 14)
    fields = scatter_about(key_list[0], (BATCH, TILES, TS, TS, C), 1.0, 6.0, ((0, 2), (1, 128)))
    cotangent = scatter_about(key_list[1], (BATCH, TILES, TS, TS, C), 1.0, 6.0, ((0, 2), (1, 128)))
    ocean_mask = draw_ocean_mask(jax.random.fold_in(key_list[13], 71), 0)
    neighbors = draw_neighbors(jax.random.fold_in(key_list[13], 71), 0)
    codes = draw_codes(jax.random.fold_in(key_list[13], 71), 0)
    dw_kernel = scatter_about(key_list[5], (BLOCKS, 49, C), 49 ** -0.5, 0.875, (), jnp.float32)
    dw_bias = scatter_about(key_list[6], (BLOCKS, C), 0.5, 3.0, (), jnp.float32)
    ln_gain = jnp.clip(1.0 + 0.1 * jax.random.normal(key_list[7], (BLOCKS, C), jnp.float32), 0.5, 1.5)
    ln_bias = scatter_about(key_list[8], (BLOCKS, C), 0.5, 3.0, (), jnp.float32)
    w_in = scatter_about(key_list[9], (BLOCKS, C, F), C ** -0.5, 0.5)
    b_in = scatter_about(key_list[10], (BLOCKS, F), 0.5, 3.0, (), jnp.float32)
    w_out = scatter_about(key_list[11], (BLOCKS, F, C), F ** -0.5, 0.25)
    b_out = scatter_about(key_list[12], (BLOCKS, C), 0.3, 2.0, (), jnp.float32)
    return {"fields": fields, "cotangent": cotangent, "ocean_mask": ocean_mask, "neighbors": neighbors, "codes": codes, "dw_kernel": dw_kernel, "dw_bias": dw_bias, "ln_gain": ln_gain, "ln_bias": ln_bias, "w_in": w_in, "b_in": b_in, "w_out": w_out, "b_out": b_out}


EPS = 1e-06
ROOT_HALF = 0.7071067811865476
INV_ROOT_TAU = 0.3989422804014327

def gelu_value(values):
    return 0.5 * values * (1.0 + lax.erf(values * ROOT_HALF))

def gelu_slope(values):
    return 0.5 * (1.0 + lax.erf(values * ROOT_HALF)) + values * INV_ROOT_TAU * jnp.exp(-0.5 * values * values)

def depthwise(padded_f, kernel, tile_width):
    summed = jnp.zeros((tile_width, tile_width, padded_f.shape[-1]), jnp.float32)
    for tap_row in range(7):
        for tap_col in range(7):
            summed = summed + kernel[tap_row * 7 + tap_col] * padded_f[tap_row:tap_row + tile_width, tap_col:tap_col + tile_width]
    return summed

def block_forward(padded, ocean_tile, params):
    kernel, conv_bias, ln_scale, ln_shift, w_first, b_first, w_second, b_second = params
    tile_width = padded.shape[0] - 6
    channels = padded.shape[-1]
    cell_count = tile_width * tile_width
    padded_f = padded.astype(jnp.float32)
    conv_out = (depthwise(padded_f, kernel, tile_width) + conv_bias).reshape(cell_count, channels)
    centred = conv_out - lax.optimization_barrier(jnp.mean(conv_out, axis=-1, keepdims=True))
    inverse = lax.rsqrt(lax.optimization_barrier(jnp.mean(centred * centred, axis=-1, keepdims=True)) + EPS)
    unit_norm = centred * inverse
    normed = (unit_norm * ln_scale + ln_shift).astype(jnp.bfloat16)
    hidden_pre = jnp.dot(normed, w_first, preferred_element_type=jnp.float32) + b_first
    hidden_act = gelu_value(hidden_pre).astype(jnp.bfloat16)
    branch = jnp.dot(hidden_act, w_second, preferred_element_type=jnp.float32) + b_second
    inflow = padded_f[3:tile_width + 3, 3:tile_width + 3].reshape(cell_count, channels)
    outflow = (inflow + ocean_tile.reshape(cell_count, 1) * branch).astype(jnp.bfloat16)
    return (outflow.reshape(tile_width, tile_width, channels), (padded_f, unit_norm, inverse, normed, hidden_pre, hidden_act))

def block_backward(saved, upstream, ocean_tile, params):
    padded_f, unit_norm, inverse, normed, hidden_pre, hidden_act = saved
    kernel, conv_bias, ln_scale, ln_shift, w_first, b_first, w_second, b_second = params
    tile_width = upstream.shape[0]
    channels = upstream.shape[-1]
    cell_count = tile_width * tile_width
    g_branch = upstream.reshape(cell_count, channels) * ocean_tile.reshape(cell_count, 1).astype(jnp.bfloat16)
    grad_b_second = lax.optimization_barrier(jnp.sum(g_branch.astype(jnp.float32), axis=0))
    grad_w_second = jnp.einsum('pf,pc->fc', hidden_act, g_branch, preferred_element_type=jnp.float32)
    g_act = jnp.einsum('pc,fc->pf', g_branch, w_second, preferred_element_type=jnp.float32)
    g_pre = g_act * gelu_slope(hidden_pre)
    grad_b_first = lax.optimization_barrier(jnp.sum(g_pre, axis=0))
    g_pre_b = g_pre.astype(jnp.bfloat16)
    grad_w_first = jnp.einsum('pc,pf->cf', normed, g_pre_b, preferred_element_type=jnp.float32)
    g_normed = jnp.einsum('pf,cf->pc', g_pre_b, w_first, preferred_element_type=jnp.float32)
    grad_scale = lax.optimization_barrier(jnp.sum(g_normed * unit_norm, axis=0))
    grad_shift = lax.optimization_barrier(jnp.sum(g_normed, axis=0))
    g_unit = g_normed * ln_scale
    g_conv = inverse * (g_unit - lax.optimization_barrier(jnp.mean(g_unit, axis=-1, keepdims=True)) - unit_norm * lax.optimization_barrier(jnp.mean(g_unit * unit_norm, axis=-1, keepdims=True)))
    grad_conv_bias = lax.optimization_barrier(jnp.sum(g_conv, axis=0))
    g_conv = g_conv.reshape(tile_width, tile_width, channels)
    kernel_terms = []
    g_padded = jnp.zeros(padded_f.shape, jnp.float32)
    for tap_row in range(7):
        for tap_col in range(7):
            window_view = padded_f[tap_row:tap_row + tile_width, tap_col:tap_col + tile_width]
            kernel_terms.append(lax.optimization_barrier(jnp.sum(g_conv * window_view, axis=(0, 1))))
            g_padded = g_padded + jnp.pad(kernel[tap_row * 7 + tap_col] * g_conv, ((tap_row, 6 - tap_row), (tap_col, 6 - tap_col), (0, 0)))
    grads = (jnp.stack(kernel_terms), grad_conv_bias, grad_scale, grad_shift, grad_w_first, grad_b_first, grad_w_second, grad_b_second)
    return (g_padded.astype(jnp.bfloat16), grads)

def canonical(tiles):
    edge_pieces = jnp.stack([jnp.rot90(tiles, quarter, axes=(2, 3))[:, :, 0:3] for quarter in range(4)], axis=2)
    corners = jnp.stack([jnp.rot90(tiles, quarter, axes=(2, 3))[:, :, 0:3, 0:3] for quarter in range(4)], axis=2)
    return (edge_pieces, corners)

def turn_half(pieces):
    return pieces[..., ::-1, ::-1, :]

def place(center, strips, blocks):
    tile_width = center.shape[2]
    padded = jnp.pad(center, ((0, 0), (0, 0), (3, 3), (3, 3), (0, 0)))
    for quarter in range(4):
        turned = jnp.rot90(padded, quarter, axes=(2, 3))
        turned = turned.at[:, :, 0:3, 3:tile_width + 3].set(strips[:, :, quarter])
        turned = turned.at[:, :, 0:3, 0:3].set(blocks[:, :, quarter])
        padded = jnp.rot90(turned, -quarter, axes=(2, 3))
    return padded

def split_padded(ct_padded):
    tile_width = ct_padded.shape[2] - 6
    strips = []
    blocks = []
    for quarter in range(4):
        turned = jnp.rot90(ct_padded, quarter, axes=(2, 3))
        strips.append(turned[:, :, 0:3, 3:tile_width + 3])
        blocks.append(turned[:, :, 0:3, 0:3])
    middle = ct_padded[:, :, 3:tile_width + 3, 3:tile_width + 3]
    return (middle, jnp.stack(strips, axis=2), jnp.stack(blocks, axis=2))

def unrotate(ct_edges, ct_corners):
    tile_width = ct_edges.shape[4]
    summed = jnp.zeros(ct_edges.shape[0:2] + (tile_width, tile_width, ct_edges.shape[5]), jnp.float32)
    for quarter in range(4):
        canvas = jnp.pad(ct_edges[:, :, quarter], ((0, 0), (0, 0), (0, tile_width - 3), (0, 0), (0, 0)))
        canvas = canvas + jnp.pad(ct_corners[:, :, quarter], ((0, 0), (0, 0), (0, tile_width - 3), (0, tile_width - 3), (0, 0)))
        summed = summed + jnp.rot90(canvas, -quarter, axes=(2, 3))
    return summed

def gather_global(tiles, neighbors, codes):
    samples, tile_count, tile_width, channels = (tiles.shape[0], tiles.shape[1], tiles.shape[2], tiles.shape[4])
    edge_pieces, corners = canonical(tiles)
    present = neighbors >= 0
    index = jnp.where(present, neighbors * 4 + codes, 0).astype(jnp.int32)
    flat_edges = edge_pieces.reshape(samples, tile_count * 4, 3, tile_width, channels)
    flat_corners = corners.reshape(samples, tile_count * 4, 3, 3, channels)
    picked_edges = jnp.take(flat_edges, index[:, 0:4].reshape(-1), axis=1).reshape(samples, tile_count, 4, 3, tile_width, channels)
    picked_corners = jnp.take(flat_corners, index[:, 4:8].reshape(-1), axis=1).reshape(samples, tile_count, 4, 3, 3, channels)
    picked_edges = jnp.where(present[None, :, 0:4, None, None, None], picked_edges, jnp.zeros((), jnp.bfloat16))
    picked_corners = jnp.where(present[None, :, 4:8, None, None, None], picked_corners, jnp.zeros((), jnp.bfloat16))
    return place(tiles, turn_half(picked_edges), turn_half(picked_corners))

def scatter_global(ct_padded, neighbors, codes):
    samples, tile_count = (ct_padded.shape[0], ct_padded.shape[1])
    middle, strips, blocks = split_padded(ct_padded)
    present = neighbors >= 0
    index = jnp.where(present, neighbors * 4 + codes, tile_count * 4).astype(jnp.int32)
    edge_terms = turn_half(strips).astype(jnp.float32).reshape(samples, tile_count * 4, -1)
    corner_terms = turn_half(blocks).astype(jnp.float32).reshape(samples, tile_count * 4, -1)
    edge_bins = jnp.zeros((samples, tile_count * 4 + 1, edge_terms.shape[-1]), jnp.float32).at[:, index[:, 0:4].reshape(-1)].add(edge_terms)
    corner_bins = jnp.zeros((samples, tile_count * 4 + 1, corner_terms.shape[-1]), jnp.float32).at[:, index[:, 4:8].reshape(-1)].add(corner_terms)
    edge_bins = edge_bins[:, 0:tile_count * 4].reshape(strips.shape)
    corner_bins = corner_bins[:, 0:tile_count * 4].reshape(blocks.shape)
    return (middle, unrotate(edge_bins, corner_bins))

def reference(fields, cotangent, ocean_mask, neighbors, codes, dw_kernel, dw_bias, ln_gain, ln_bias, w_in, b_in, w_out, b_out):
    samples, tile_count, tile_width, channels = (fields.shape[0], fields.shape[1], fields.shape[2], fields.shape[4])
    ocean_f = ocean_mask.astype(jnp.float32)
    ocean_flat = jnp.broadcast_to(ocean_f[None], (samples,) + ocean_f.shape).reshape(-1, tile_width, tile_width)
    current = fields
    inputs = []
    for block_idx in range(BLOCKS):
        params = (dw_kernel[block_idx], dw_bias[block_idx], ln_gain[block_idx], ln_bias[block_idx], w_in[block_idx], b_in[block_idx], w_out[block_idx], b_out[block_idx])
        padded = gather_global(current, neighbors, codes)
        inputs.append(padded)
        flat_tiles = padded.reshape(-1, tile_width + 6, tile_width + 6, channels)
        current = lax.map(lambda element: block_forward(element[0], element[1], params)[0], (flat_tiles, ocean_flat)).reshape(fields.shape)
    out_fields = current
    upstream = cotangent
    block_grads = [None] * BLOCKS
    for block_idx in range(BLOCKS - 1, -1, -1):
        params = (dw_kernel[block_idx], dw_bias[block_idx], ln_gain[block_idx], ln_bias[block_idx], w_in[block_idx], b_in[block_idx], w_out[block_idx], b_out[block_idx])
        flat_tiles = inputs[block_idx].reshape(-1, tile_width + 6, tile_width + 6, channels)

        def per_tile(carried, element):
            saved = block_forward(element[0], element[1], params)[1]
            g_pad, tile_terms = block_backward(saved, element[2], element[1], params)
            return (jax.tree.map(jnp.add, carried, tile_terms), g_pad)
        zero_grads = tuple((jnp.zeros(member.shape, jnp.float32) for member in params))
        sums, g_flat = lax.scan(per_tile, zero_grads, (flat_tiles, ocean_flat, upstream.reshape(-1, tile_width, tile_width, channels)))
        middle, returned = scatter_global(g_flat.reshape(inputs[block_idx].shape), neighbors, codes)
        upstream = (upstream.astype(jnp.float32) + middle.astype(jnp.float32) + returned).astype(jnp.bfloat16)
        block_grads[block_idx] = sums
    scale = 1.0 / math.sqrt(CELLS)
    stacked = [jnp.stack([block_grads[block_idx][member] for block_idx in range(BLOCKS)]) * scale for member in range(8)]
    return (out_fields, upstream, stacked[0], stacked[1], stacked[2], stacked[3], stacked[4], stacked[5], stacked[6], stacked[7])
```

```python
import math

import jax
import jax.numpy as jnp
import numpy as np
from jax import lax
from jax.experimental import pallas as pl
from jax.experimental.pallas import tpu as pltpu
from jax.sharding import PartitionSpec as P

RANGE = 2
BLOCKS = 2
WINDOW = 2 * RANGE + 1
OFFSETS = (-2, -1, 1, 2)

EPS = 1e-06
ROOT_HALF = 0.7071067811865476
INV_ROOT_TAU = 0.3989422804014327

TS = 16
CELLS = TS * TS
C = 128
F = 512
FC = 256
SLOTS = 2
RIM = 160
NEAR = WINDOW * SLOTS * RIM
RING_S = 320
RING_T = 272
GROWS = 1152
SMALL = 1024
VMEM = 48 * 1024 * 1024

f32 = jnp.float32
bf16 = jnp.bfloat16


def rim_of_cell():
    rim = np.full((TS, TS), -1, np.int32)
    for i in range(TS):
        for j in range(TS):
            if i < 3:
                rim[i, j] = i * TS + j
            elif i >= 13:
                rim[i, j] = 48 + (i - 13) * TS + j
            elif j < 3:
                rim[i, j] = 96 + (i - 3) * 6 + j
            elif j >= 13:
                rim[i, j] = 96 + (i - 3) * 6 + 3 + (j - 13)
    return rim


def ring_tables():
    rim = rim_of_cell()
    entry = np.full((22 * 22,), -1, np.int32)
    source = np.zeros((22 * 22, 4), np.int32)
    frame = np.arange(22 * 22).reshape(22, 22)
    for q in range(4):
        turned = np.rot90(frame, q)
        edge, corner = turned[0:3, 3:19], turned[0:3, 0:3]
        entry[edge] = q
        entry[corner] = q + 4
        for code in range(4):
            piece = np.rot90(rim, code)
            source[edge, code] = piece[0:3][::-1, ::-1]
            source[corner, code] = piece[0:3, 0:3][::-1, ::-1]
    return entry.reshape(22, 22), source.reshape(22, 22, 4)


def ordered_tables(order):
    entry, source = ring_tables()
    rows = len(order)
    one_hot = np.zeros((rows, 8), np.int32)
    tab = np.zeros((rows, 4), np.int32)
    away = np.zeros((rows,), np.int32)
    for r, at in enumerate(order):
        if at is None or entry[at] < 0:
            away[r] = -1000000
        else:
            one_hot[r, entry[at]] = 1
            tab[r] = source[at]
    return one_hot, tab, away


def order_s():
    out = []
    for rows in (range(0, 3), range(19, 22)):
        for p in rows:
            out += [(p, cc - 5) if 0 <= cc - 5 < 22 else None for cc in range(32)]
    for p in range(3, 19):
        out += [(p, 19), (p, 20), (p, 21), None, None, (p, 0), (p, 1), (p, 2)]
    return out


def order_t():
    out = []
    for rows in (range(0, 3), range(19, 22)):
        for p in rows:
            out += [(p, cc) if cc < 22 else None for cc in range(24)]
    for p in range(3, 19):
        out += [(p, 0), (p, 1), (p, 2), (p, 19), (p, 20), (p, 21), None, None]
    return out


def rim_select():
    sel = np.zeros((RIM, CELLS), np.float32)
    rim = rim_of_cell().reshape(-1)
    for cell in range(CELLS):
        if rim[cell] >= 0:
            sel[rim[cell], cell] = 1.0
    return sel


def dot(a, b):
    return lax.dot_general(a, b, (((1,), (0,)), ((), ())), preferred_element_type=f32)


def dot_nt(a, b):
    return lax.dot_general(a, b, (((1,), (1,)), ((), ())), preferred_element_type=f32)


def dot_tn(a, b):
    return lax.dot_general(a, b, (((0,), (0,)), ((), ())), preferred_element_type=f32)


def assemble(pad_ref, t, ring, center):
    pad_ref[t, 0:3] = ring[0:96].reshape(3, 32, C)
    pad_ref[t, 19:22] = ring[96:192].reshape(3, 32, C)
    sides = ring[192:320].reshape(TS, 8, C)
    pad_ref[t, 3:19, 0:8] = sides
    pad_ref[t, 3:19, 24:32] = sides
    pad_ref[t, 3:19, 8:24] = center.astype(f32).reshape(TS, TS, C)


def depthwise(pad_ref, k_ref, bias, conv_ref):
    for t in range(SLOTS):
        for half in range(2):
            total = jnp.broadcast_to(bias.reshape(1, 1, C), (8, TS, C))
            for e in range(7):
                moved = pad_ref[t, 8 * half : 8 * half + 14, 5 + e : 21 + e, :]
                for a in range(7):
                    tap = k_ref[7 * a + e : 7 * a + e + 1, :].reshape(1, 1, C)
                    total = total + tap * moved[a : a + 8]
            at = t * CELLS + half * 128
            conv_ref[at : at + 128] = total.reshape(128, C)


def normalise(conv, gain, shift):
    centred = conv - jnp.mean(conv, axis=-1, keepdims=True)
    inverse = lax.rsqrt(jnp.mean(centred * centred, axis=-1, keepdims=True) + EPS)
    unit = centred * inverse
    return unit, inverse, (unit * gain + shift).astype(bf16)


def spread(g_conv, gc_ref, k_ref, g_ref):
    for t in range(SLOTS):
        gc_ref[t, :, 0:8] = jnp.zeros((TS, 8, C), f32)
        gc_ref[t, :, 24:32] = jnp.zeros((TS, 8, C), f32)
        gc_ref[t, :, 8:24] = g_conv[t * CELLS : (t + 1) * CELLS].reshape(TS, TS, C)
    for t in range(SLOTS):
        for first, last in ((0, 6), (6, 11), (11, 16), (16, 22)):
            totals = [None] * (last - first)
            low, high = max(0, first - 6), min(TS, last)
            for e in range(7):
                moved = gc_ref[t, low:high, 8 - e : 32 - e, :]
                for a in range(7):
                    tap = k_ref[7 * a + e : 7 * a + e + 1, :]
                    for p in range(first, last):
                        r = p - a
                        if 0 <= r < TS:
                            term = tap * moved[r - low]
                            was = totals[p - first]
                            totals[p - first] = term if was is None else was + term
            for p in range(first, last):
                g_ref[t, p] = totals[p - first]


def ring_out(g_ref, ring_ref):
    for t in range(SLOTS):
        at = t * RING_T
        ring_ref[at : at + 72] = g_ref[t, 0:3].reshape(72, C).astype(bf16)
        ring_ref[at + 72 : at + 144] = g_ref[t, 19:22].reshape(72, C).astype(bf16)
        left = g_ref[t, 3:19, 0:8]
        right = g_ref[t, 3:19, 16:24]
        column = lax.broadcasted_iota(jnp.int32, (TS, 8, C), 1)
        ring_ref[at + 144 : at + 272] = jnp.where(column < 3, left, right).reshape(128, C).astype(bf16)


def kernel_terms(pad_ref, gc_ref, grads_ref):
    for e in range(7):
        sums = [None] * 7
        for t in range(SLOTS):
            for half in range(2):
                moved = pad_ref[t, 8 * half : 8 * half + 14, 5 + e : 21 + e, :]
                here = gc_ref[t, 8 * half : 8 * half + 8, 8:24]
                for a in range(7):
                    part = jnp.sum(here * moved[a : a + 8], axis=0)
                    part = part[0:8] + part[8:16]
                    sums[a] = part if sums[a] is None else sums[a] + part
        for a in range(7):
            at = SMALL + 7 * a + e
            grads_ref[at : at + 1] = jnp.sum(sums[a], axis=0, keepdims=True)


def column_sum(x):
    return jnp.sum(x, axis=0, keepdims=True)


def backward(unit, inverse, normed, upstream, mask, wts, grads_ref, out_branch):
    gain_ref, w_in_ref, b_in_ref, w_out_ref = wts
    g_branch = upstream * mask.astype(bf16)
    grads_ref[SMALL + 49 :] = jnp.zeros((GROWS - SMALL - 49, C), f32)
    g_normed = None
    branch = None
    for at in range(0, F, FC):
        w1 = w_in_ref[:, at : at + FC]
        w2 = w_out_ref[at : at + FC, :]
        pre = dot(normed, w1) + b_in_ref[0:1, at : at + FC]
        error = lax.erf(pre * ROOT_HALF)
        half = 0.5 * (1.0 + error)
        act = (pre * half).astype(bf16)
        if out_branch:
            part = dot(act, w2)
            branch = part if branch is None else branch + part
        slope = half + pre * INV_ROOT_TAU * jnp.exp(-0.5 * pre * pre)
        g_pre = dot_nt(g_branch, w2) * slope
        g_bias = column_sum(g_pre)
        g_pre_b = g_pre.astype(bf16)
        g_w1 = dot_tn(normed, g_pre_b)
        for c0 in range(0, FC, C):
            grads_ref[at + c0 : at + c0 + C] = g_w1[:, c0 : c0 + C]
            row = SMALL + 52 + (at + c0) // C
            grads_ref[row : row + 1] = g_bias[:, c0 : c0 + C]
        grads_ref[512 + at : 512 + at + FC] = dot_tn(act, g_branch)
        part = dot_nt(g_pre_b, w1)
        g_normed = part if g_normed is None else g_normed + part
    g_unit = g_normed * gain_ref[0:1]
    g_conv = inverse * (
        g_unit
        - jnp.mean(g_unit, axis=-1, keepdims=True)
        - unit * jnp.mean(g_unit * unit, axis=-1, keepdims=True)
    )
    grads_ref[SMALL + 49 : SMALL + 50] = column_sum(g_conv)
    grads_ref[SMALL + 50 : SMALL + 51] = column_sum(g_normed * unit)
    grads_ref[SMALL + 51 : SMALL + 52] = column_sum(g_normed)
    grads_ref[SMALL + 56 : SMALL + 57] = column_sum(g_branch.astype(f32))
    return g_conv, branch


def put_pieces(st_ref, ring_ref, piece_refs):
    bins = dot(st_ref[...], ring_ref[...]).astype(bf16)
    for o in range(WINDOW):
        piece_refs[o][...] = bins[o * SLOTS * RIM : (o + 1) * SLOTS * RIM]


def put_base(g_ref, upstream, base_ref):
    for t in range(SLOTS):
        center = g_ref[t, 3:19, 3:19, :].reshape(CELLS, C).astype(bf16).astype(f32)
        base_ref[t] = upstream[t * CELLS : (t + 1) * CELLS] + center


def combined(base_ref, pieces, expand_ref):
    out = []
    for t in range(SLOTS):
        joined = jnp.concatenate([p[t * RIM : (t + 1) * RIM] for p in pieces], axis=0)
        out.append((base_ref[t] + dot(expand_ref[...], joined)).astype(bf16))
    return out


def first_kernel(own, m2, m1, p1, p2, sel, rim_sel, mask, k, db, gain, shift, w_in, b_in, w_out, b_out,
                 out, rims, pad, conv, near):
    for o, ref in enumerate((m2, m1, own, p1, p2)):
        for t in range(SLOTS):
            at = (o * SLOTS + t) * RIM
            near[at : at + RIM] = dot(rim_sel[...], ref[t]).astype(bf16)
    ring = dot(sel[...], near[...])
    for t in range(SLOTS):
        assemble(pad, t, ring[t * RING_S : (t + 1) * RING_S], own[t])
    depthwise(pad, k, db[0:1], conv)
    unit, inverse, normed = normalise(conv[...], gain[0:1], shift[0:1])
    branch = None
    for at in range(0, F, FC):
        pre = dot(normed, w_in[:, at : at + FC]) + b_in[0:1, at : at + FC]
        act = (0.5 * pre * (1.0 + lax.erf(pre * ROOT_HALF))).astype(bf16)
        part = dot(act, w_out[at : at + FC, :])
        branch = part if branch is None else branch + part
    branch = branch + b_out[0:1]
    for t in range(SLOTS):
        lo, hi = t * CELLS, (t + 1) * CELLS
        value = (own[t].astype(f32) + mask[lo:hi] * branch[lo:hi]).astype(bf16)
        out[t] = value
        rims[t * RIM : (t + 1) * RIM] = dot(rim_sel[...], value).astype(bf16)


def middle_kernel(own, r_own, m2, m1, p1, p2, sel, sel_t, cot, mask, k, db, gain, shift, w_in, b_in, w_out, b_out,
                  out, q0, q1, q2, q3, q4, base, grads, near, pad, conv, gc, g, ring_b):
    for o, ref in enumerate((m2, m1, r_own, p1, p2)):
        near[o * SLOTS * RIM : (o + 1) * SLOTS * RIM] = ref[...]
    ring = dot(sel[...], near[...])
    for t in range(SLOTS):
        assemble(pad, t, ring[t * RING_S : (t + 1) * RING_S], own[t])
    depthwise(pad, k, db[0:1], conv)
    unit, inverse, normed = normalise(conv[...], gain[0:1], shift[0:1])
    upstream = cot[...].reshape(SLOTS * CELLS, C)
    g_conv, branch = backward(unit, inverse, normed, upstream, mask[...], (gain, w_in, b_in, w_out), grads, True)
    branch = branch + b_out[0:1]
    for t in range(SLOTS):
        lo, hi = t * CELLS, (t + 1) * CELLS
        out[t] = (own[t].astype(f32) + mask[lo:hi] * branch[lo:hi]).astype(bf16)
    spread(g_conv, gc, k, g)
    ring_out(g, ring_b)
    put_pieces(sel_t, ring_b, (q0, q1, q2, q3, q4))
    put_base(g, upstream.astype(f32), base)
    kernel_terms(pad, gc, grads)


def last_kernel(base_in, i0, i1, i2, i3, i4, expand, pad, conv, sel_t, mask, k, gain, shift, w_in, b_in, w_out,
                q0, q1, q2, q3, q4, base, grads, gc, g, ring_b):
    parts = combined(base_in, [r[...] for r in (i0, i1, i2, i3, i4)], expand)
    upstream = jnp.concatenate(parts, axis=0)
    unit, inverse, normed = normalise(conv[...], gain[0:1], shift[0:1])
    g_conv, _ = backward(unit, inverse, normed, upstream, mask[...], (gain, w_in, b_in, w_out), grads, False)
    spread(g_conv, gc, k, g)
    ring_out(g, ring_b)
    put_pieces(sel_t, ring_b, (q0, q1, q2, q3, q4))
    put_base(g, upstream.astype(f32), base)
    kernel_terms(pad, gc, grads)


def closing_kernel(base_in, i0, i1, i2, i3, i4, expand, out):
    parts = combined(base_in, [r[...] for r in (i0, i1, i2, i3, i4)], expand)
    for t in range(SLOTS):
        out[t] = parts[t]


def unpack_kernel(scale, packed, dw, dwb, gain, shift, w_in, b_in, w_out, b_out):
    for b in range(BLOCKS):
        at = b * GROWS
        value = packed[at : at + GROWS].astype(f32) * scale
        for c0 in range(0, F, C):
            w_in[b, :, c0 : c0 + C] = value[c0 : c0 + C]
            row = SMALL + 52 + c0 // C
            b_in[b : b + 1, c0 : c0 + C] = value[row : row + 1]
        w_out[b] = value[512:1024]
        dw[b] = value[SMALL : SMALL + 49]
        dwb[b : b + 1] = value[SMALL + 49 : SMALL + 50]
        gain[b : b + 1] = value[SMALL + 50 : SMALL + 51]
        shift[b : b + 1] = value[SMALL + 51 : SMALL + 52]
        b_out[b : b + 1] = value[SMALL + 56 : SMALL + 57]


def shape(dims, kind):
    return jax.ShapeDtypeStruct(dims, kind)


def call(kernel, outs, args, scratch=(), flops=1000000, name=None):
    vmem = pl.BlockSpec(memory_space=pltpu.VMEM)
    size = sum(math.prod(a.shape) * a.dtype.itemsize for a in list(args) + list(outs))
    return pl.pallas_call(
        kernel,
        out_shape=outs,
        in_specs=[vmem] * len(args),
        out_specs=[vmem] * len(outs),
        scratch_shapes=list(scratch),
        compiler_params=pltpu.CompilerParams(vmem_limit_bytes=VMEM),
        cost_estimate=pl.CostEstimate(flops=flops, bytes_accessed=size, transcendentals=0),
        name=name,
    )(*args)


def shift_by(x, by):
    n = lax.axis_size("space")
    return lax.ppermute(x, "space", [(i, (i + by) % n) for i in range(n)])


def strides(axis):
    return {"core": (1, 2), "z": (2, 4), "x": (8, 4), "y": (32, 4)}[axis]


def coordinate(axis):
    stride, extent = strides(axis)
    return (lax.axis_index("space") // stride) % extent


def along(x, axis, move):
    if axis == "dp":
        return lax.ppermute(x, "dp", [(0, 1), (1, 0)])
    stride, extent = strides(axis)
    pairs = []
    for i in range(lax.axis_size("space")):
        c = (i // stride) % extent
        pairs.append((i, i + (move(c) - c) * stride))
    return lax.ppermute(x, "space", pairs)


def scatter_sum(x, axis, kind):
    extent = strides(axis)[1]
    me = coordinate(axis)
    parts = x.reshape((extent, -1, C))
    total = lax.dynamic_index_in_dim(parts, me, 0, keepdims=False)
    for d in range(1, extent):
        piece = lax.dynamic_index_in_dim(parts, (me + d) % extent, 0, keepdims=False).astype(kind)
        total = total + along(piece, axis, lambda c: (c + d) % extent).astype(f32)
    return total


def exchange_sum(x, axis, mask):
    return x + along(x, axis, lambda c: c ^ mask)


def collect(x, axis):
    extent = strides(axis)[1]
    me = coordinate(axis)
    out = lax.dynamic_update_index_in_dim(jnp.zeros((extent,) + x.shape, x.dtype), x, me, 0)
    for d in range(1, extent):
        got = along(x, axis, lambda c: (c + d) % extent)
        out = lax.dynamic_update_index_in_dim(out, got, (me - d) % extent, 0)
    return out.reshape(-1, C)


def reduced(g):
    x = scatter_sum(g, "core", f32)
    x = scatter_sum(x, "x", bf16)
    x = scatter_sum(x, "y", bf16)
    x = exchange_sum(x, "z", 1)
    x = exchange_sum(x, "z", 2)
    x = exchange_sum(x, "dp", 1)
    x = x.astype(bf16)
    x = collect(x, "y")
    x = collect(x, "x")
    return collect(x, "core")


def selectors(neighbors, codes):
    n = lax.axis_size("space")
    distance = jnp.mod(jnp.floor_divide(neighbors, SLOTS) - lax.axis_index("space"), n)
    distance = jnp.where(distance > n // 2, distance - n, distance)
    start = (distance + RANGE) * (SLOTS * RIM) + jnp.mod(neighbors, SLOTS) * RIM
    start = jnp.where(neighbors >= 0, start, -1000000)

    def index(order):
        one_hot, tab, away = ordered_tables(order)
        begin = jnp.sum(start[:, None, :] * one_hot[None], axis=-1)
        code = jnp.sum(codes[:, None, :] * one_hot[None], axis=-1)
        inside = sum(jnp.where(code == c, tab[None, :, c], 0) for c in range(4))
        return (begin + inside + away[None]).reshape(-1)

    cells = jnp.arange(NEAR, dtype=jnp.int32)
    sel = (index(order_s())[:, None] == cells[None, :]).astype(bf16)
    sel_t = (cells[:, None] == index(order_t())[None, :]).astype(bf16)
    return sel, sel_t


def local(fields, cotangent, ocean_mask, neighbors, codes, dw_kernel, dw_bias, ln_gain, ln_bias, w_in, b_in, w_out,
          b_out):
    dims = fields.shape
    own = fields.reshape(SLOTS, CELLS, C)
    raw = [shift_by(own, -o) for o in OFFSETS]
    sel, sel_t = selectors(neighbors, codes)
    mask = ocean_mask.astype(f32).reshape(SLOTS * CELLS, 1)
    rim_np = rim_select()
    rim_sel = jnp.asarray(rim_np, bf16)
    expand = jnp.asarray(np.tile(rim_np.T, (1, WINDOW)), bf16)

    def params(b):
        return (dw_kernel[b], dw_bias[b : b + 1], ln_gain[b : b + 1], ln_bias[b : b + 1], w_in[b], b_in[b : b + 1],
                w_out[b], b_out[b : b + 1])

    tile = (SLOTS, CELLS, C)
    flat = (SLOTS * CELLS, C)
    padded = (SLOTS, 22, 32, C)
    rims_shape = shape((SLOTS * RIM, C), bf16)
    out0, rims, pad0, conv0 = call(
        first_kernel,
        [shape(tile, bf16), rims_shape, shape(padded, f32), shape(flat, f32)],
        [own, *raw, sel, rim_sel, mask, *params(0)],
        [pltpu.VMEM((NEAR, C), bf16)],
        flops=2000000000, name="block0_forward",
    )
    got = [shift_by(rims, -o) for o in OFFSETS]
    back = [
        pltpu.VMEM((SLOTS, TS, 32, C), f32),
        pltpu.VMEM((SLOTS, 22, 24, C), f32),
        pltpu.VMEM((SLOTS * RING_T, C), bf16),
    ]
    out1, q0, q1, q2, q3, q4, base1, grads1 = call(
        middle_kernel,
        [shape(tile, bf16)] + [rims_shape] * 5 + [shape(tile, f32), shape((GROWS, C), f32)],
        [out0, rims, *got, sel, sel_t, cotangent.reshape(tile), mask, *params(1)],
        [pltpu.VMEM((NEAR, C), bf16), pltpu.VMEM(padded, f32), pltpu.VMEM(flat, f32)] + back,
        flops=4000000000, name="block1_both",
    )
    pieces = [q2] + [shift_by(q, o) for q, o in zip((q0, q1, q3, q4), OFFSETS)]
    k0 = params(0)
    q0, q1, q2, q3, q4, base0, grads0 = call(
        last_kernel,
        [rims_shape] * 5 + [shape(tile, f32), shape((GROWS, C), f32)],
        [base1, *pieces, expand, pad0, conv0, sel_t, mask, k0[0], k0[2], k0[3], k0[4], k0[5], k0[6]],
        back,
        flops=3000000000, name="block0_backward",
    )
    pieces = [q2] + [shift_by(q, o) for q, o in zip((q0, q1, q3, q4), OFFSETS)]
    (field_grad,) = call(
        closing_kernel, [shape(tile, bf16)], [base0, *pieces, expand], flops=100000000, name="closing"
    )
    packed = reduced(jnp.concatenate([grads0, grads1], axis=0))
    scale = 1.0 / math.sqrt(SLOTS * CELLS * lax.axis_size("dp") * lax.axis_size("space"))
    grads = call(
        lambda *refs: unpack_kernel(scale, *refs),
        [
            shape((BLOCKS, 49, C), f32), shape((BLOCKS, C), f32), shape((BLOCKS, C), f32), shape((BLOCKS, C), f32),
            shape((BLOCKS, C, F), f32), shape((BLOCKS, F), f32), shape((BLOCKS, F, C), f32), shape((BLOCKS, C), f32),
        ],
        [packed], flops=1000000, name="unpack",
    )
    return (out1.reshape(dims), field_grad.reshape(dims), *grads)


def solution(mesh):
    placed = (
        P("dp", "space", None, None, None),
        P("dp", "space", None, None, None),
        P("space", None, None),
        P("space", None),
        P("space", None),
    ) + (P(),) * 8
    return jax.shard_map(
        local,
        mesh=mesh,
        in_specs=placed,
        out_specs=(P("dp", "space", None, None, None), P("dp", "space", None, None, None)) + (P(),) * 8,
        check_vma=False,
    )
```

```python
import math

import jax
import jax.numpy as jnp
import numpy as np
from jax import lax
from jax.experimental import pallas as pl
from jax.experimental.pallas import tpu as pltpu
from jax.sharding import PartitionSpec as P

RANGE = 2
BLOCKS = 2
WINDOW = 2 * RANGE + 1
OFFSETS = (-2, -1, 1, 2)

EPS = 1e-06
ROOT_HALF = 0.7071067811865476
INV_ROOT_TAU = 0.3989422804014327

TS = 16
CELLS = TS * TS
C = 128
F = 512
FC = 256
SLOTS = 2
RIM = 160
RING_S = 320
RING_T = 272
BLOCK = 64
TILE_ROWS = 4 * BLOCK
BINS = WINDOW * SLOTS * TILE_ROWS + BLOCK
AT_CELL, AT_RIM, AT_PUT, AT_TAKE, AT_OUT, AT_END = 0, 256, 512, 832, 1104, 1264
GROWS = 1152
SMALL = 1024
VMEM = 14 * 1024 * 1024

f32 = jnp.float32
bf16 = jnp.bfloat16


def rim_of_cell():
    rim = np.full((TS, TS), -1, np.int32)
    for i in range(TS):
        for j in range(TS):
            if i < 3:
                rim[i, j] = i * TS + j
            elif i >= 13:
                rim[i, j] = 48 + (i - 13) * TS + j
            elif j < 3:
                rim[i, j] = 96 + (i - 3) * 6 + j
            elif j >= 13:
                rim[i, j] = 96 + (i - 3) * 6 + 3 + (j - 13)
    return rim


def pieces_of(code):
    turned = np.rot90(np.arange(CELLS).reshape(TS, TS), code)
    out = np.full((BLOCK,), -1, np.int32)
    out[0:48] = turned[0:3][::-1, ::-1].reshape(-1)
    out[48:57] = turned[0:3, 0:3][::-1, ::-1].reshape(-1)
    return out


def frame_positions():
    frame = np.arange(22 * 22).reshape(22, 22)
    row = np.full((22 * 22,), -1, np.int32)
    for q in range(4):
        turned = np.rot90(frame, q)
        row[turned[0:3, 3:19].reshape(-1)] = q * 48 + np.arange(48)
        row[turned[0:3, 0:3].reshape(-1)] = 192 + q * 16 + np.arange(9)
    return row.reshape(22, 22)


def order_s():
    out = []
    for rows in (range(0, 3), range(19, 22)):
        for p in rows:
            out += [(p, cc - 5) if 0 <= cc - 5 < 22 else None for cc in range(32)]
    for p in range(3, 19):
        out += [(p, 19), (p, 20), (p, 21), None, None, (p, 0), (p, 1), (p, 2)]
    return out


def order_t():
    out = []
    for rows in (range(0, 3), range(19, 22)):
        for p in rows:
            out += [(p, cc) if cc < 22 else None for cc in range(24)]
    for p in range(3, 19):
        out += [(p, 0), (p, 1), (p, 2), (p, 19), (p, 20), (p, 21), None, None]
    return out


def fixed_rows():
    rim = rim_of_cell().reshape(-1)
    cell_of_rim = np.full((RIM,), -1, np.int32)
    for cell in range(CELLS):
        if rim[cell] >= 0:
            cell_of_rim[rim[cell]] = cell
    codes = np.concatenate([pieces_of(code) for code in range(4)])
    from_rim = np.where(codes >= 0, rim[codes], -1)
    at = frame_positions()
    put = np.array([-1 if p is None else at[p] for p in order_s()], np.int32)
    take = np.array([-1 if p is None else at[p] for p in order_t()], np.int32)
    return np.concatenate([codes, from_rim, put, take, cell_of_rim]).astype(np.int32)


def dot(a, b):
    return lax.dot_general(a, b, (((1,), (0,)), ((), ())), preferred_element_type=f32)


def dot_nt(a, b):
    return lax.dot_general(a, b, (((1,), (1,)), ((), ())), preferred_element_type=f32)


def dot_tn(a, b):
    return lax.dot_general(a, b, (((0,), (0,)), ((), ())), preferred_element_type=f32)


def assemble(pad_ref, t, ring, center):
    pad_ref[t, 0:3] = ring[0:96].reshape(3, 32, C)
    pad_ref[t, 19:22] = ring[96:192].reshape(3, 32, C)
    sides = ring[192:320].reshape(TS, 8, C)
    pad_ref[t, 3:19, 0:8] = sides
    pad_ref[t, 3:19, 24:32] = sides
    pad_ref[t, 3:19, 8:24] = center.astype(f32).reshape(TS, TS, C)


def depthwise(pad_ref, k_ref, b, bias, conv_ref):
    for t in range(SLOTS):
        for half in range(2):
            total = jnp.broadcast_to(bias.reshape(1, 1, C), (8, TS, C))
            for e in range(7):
                moved = pad_ref[t, 8 * half : 8 * half + 14, 5 + e : 21 + e, :]
                for a in range(7):
                    tap = k_ref[b, 7 * a + e : 7 * a + e + 1, :].reshape(1, 1, C)
                    total = total + tap * moved[a : a + 8]
            at = t * CELLS + half * 128
            conv_ref[at : at + 128] = total.reshape(128, C)


def normalise(conv, gain, shift):
    centred = conv - jnp.mean(conv, axis=-1, keepdims=True)
    inverse = lax.rsqrt(jnp.mean(centred * centred, axis=-1, keepdims=True) + EPS)
    unit = centred * inverse
    return unit, inverse, (unit * gain + shift).astype(bf16)


def spread(g_conv, gc_ref, k_ref, b, g_ref):
    for t in range(SLOTS):
        gc_ref[t, :, 0:8] = jnp.zeros((TS, 8, C), f32)
        gc_ref[t, :, 24:32] = jnp.zeros((TS, 8, C), f32)
        gc_ref[t, :, 8:24] = g_conv[t * CELLS : (t + 1) * CELLS].reshape(TS, TS, C)
    for t in range(SLOTS):
        for first, last in ((0, 6), (6, 11), (11, 16), (16, 22)):
            totals = [None] * (last - first)
            low, high = max(0, first - 6), min(TS, last)
            for e in range(7):
                moved = gc_ref[t, low:high, 8 - e : 32 - e, :]
                for a in range(7):
                    tap = k_ref[b, 7 * a + e : 7 * a + e + 1, :]
                    for p in range(first, last):
                        r = p - a
                        if 0 <= r < TS:
                            term = tap * moved[r - low]
                            was = totals[p - first]
                            totals[p - first] = term if was is None else was + term
            for p in range(first, last):
                g_ref[t, p] = totals[p - first]


def ring_out(g_ref, ring_ref):
    for t in range(SLOTS):
        at = t * RING_T
        ring_ref[at : at + 72] = g_ref[t, 0:3].reshape(72, C).astype(bf16)
        ring_ref[at + 72 : at + 144] = g_ref[t, 19:22].reshape(72, C).astype(bf16)
        left = g_ref[t, 3:19, 0:8]
        right = g_ref[t, 3:19, 16:24]
        column = lax.broadcasted_iota(jnp.int32, (TS, 8, C), 1)
        ring_ref[at + 144 : at + 272] = jnp.where(column < 3, left, right).reshape(128, C).astype(bf16)


def kernel_terms(pad_ref, gc_ref, grads_ref):
    for e in range(7):
        sums = [None] * 7
        for t in range(SLOTS):
            for half in range(2):
                moved = pad_ref[t, 8 * half : 8 * half + 14, 5 + e : 21 + e, :]
                here = gc_ref[t, 8 * half : 8 * half + 8, 8:24]
                for a in range(7):
                    part = jnp.sum(here * moved[a : a + 8], axis=0)
                    part = part[0:8] + part[8:16]
                    sums[a] = part if sums[a] is None else sums[a] + part
        for a in range(7):
            at = SMALL + 7 * a + e
            grads_ref[at : at + 1] = jnp.sum(sums[a], axis=0, keepdims=True)


def column_sum(x):
    return jnp.sum(x, axis=0, keepdims=True)


def bias_in(small_ref, b, at):
    first = 4 + at // C
    return jnp.concatenate([small_ref[b, r : r + 1] for r in range(first, first + FC // C)], axis=1)


def pointwise_back(b, unit, inverse, normed, g_branch, wts, kept):
    small_ref, w_in_ref, w_out_ref = wts
    act_ref, g_pre_ref, g_bias_ref, g_normed_ref = kept
    g_normed = None
    for at in range(0, F, FC):
        w1 = w_in_ref[b, 0:C, at : at + FC]
        w2 = w_out_ref[b, at : at + FC, :]
        pre = dot(normed, w1) + bias_in(small_ref, b, at)
        half = 0.5 * (1.0 + lax.erf(pre * ROOT_HALF))
        act_ref[:, at : at + FC] = (pre * half).astype(bf16)
        slope = half + pre * INV_ROOT_TAU * jnp.exp(-0.5 * pre * pre)
        g_pre = dot_nt(g_branch, w2) * slope
        g_bias_ref[0:1, at : at + FC] = column_sum(g_pre)
        g_pre_b = g_pre.astype(bf16)
        g_pre_ref[:, at : at + FC] = g_pre_b
        part = dot_nt(g_pre_b, w1)
        g_normed = part if g_normed is None else g_normed + part
    g_normed_ref[...] = g_normed
    g_unit = g_normed * small_ref[b, 1:2]
    return inverse * (
        g_unit
        - jnp.mean(g_unit, axis=-1, keepdims=True)
        - unit * jnp.mean(g_unit * unit, axis=-1, keepdims=True)
    )


def weight_terms(pad_ref, gc_ref, unit, normed, g_branch, kept, grads_ref):
    act_ref, g_pre_ref, g_bias_ref, g_normed_ref = kept
    grads_ref[SMALL + 49 : GROWS] = jnp.zeros((GROWS - SMALL - 49, C), f32)
    for at in range(0, F, FC):
        g_w1 = dot_tn(normed, g_pre_ref[:, at : at + FC])
        for c0 in range(0, FC, C):
            grads_ref[at + c0 : at + c0 + C] = g_w1[:, c0 : c0 + C]
            row = SMALL + 52 + (at + c0) // C
            grads_ref[row : row + 1] = g_bias_ref[0:1, at + c0 : at + c0 + C]
        grads_ref[512 + at : 512 + at + FC] = dot_tn(act_ref[:, at : at + FC], g_branch)
    g_normed = g_normed_ref[...]
    g_conv_sum = sum(jnp.sum(gc_ref[t, :, 8:24].reshape(CELLS, C), axis=0, keepdims=True) for t in range(SLOTS))
    grads_ref[SMALL + 49 : SMALL + 50] = g_conv_sum
    grads_ref[SMALL + 50 : SMALL + 51] = column_sum(g_normed * unit)
    grads_ref[SMALL + 51 : SMALL + 52] = column_sum(g_normed)
    grads_ref[SMALL + 56 : SMALL + 57] = column_sum(g_branch.astype(f32))
    kernel_terms(pad_ref, gc_ref, grads_ref)


def picked(start, canon, t):
    parts = []
    for q in range(8):
        first = pl.multiple_of(start[t, q], BLOCK)
        parts.append(canon[pl.ds(first, 48), :] if q < 4 else canon[pl.ds(first + 48, 16), :])
    return jnp.concatenate(parts, axis=0)


def put_pieces(start, fixed, ring_ref, bins, piece_refs):
    bins[...] = jnp.zeros((BINS, C), f32)
    for t in range(SLOTS):
        ring = ring_ref[t * RING_T : (t + 1) * RING_T]
        parts = dot_tn(fixed[AT_TAKE:AT_OUT, :], ring)
        for q in range(8):
            first = pl.multiple_of(start[t, q], BLOCK)
            if q < 4:
                bins[pl.ds(first, 48), :] += parts[q * 48 : (q + 1) * 48]
            else:
                bins[pl.ds(first + 48, 16), :] += parts[192 + (q - 4) * 16 : 208 + (q - 4) * 16]
    to_rim = fixed[AT_RIM:AT_PUT, 0:RIM]
    for o in range(WINDOW):
        for t in range(SLOTS):
            at = (o * SLOTS + t) * TILE_ROWS
            given = bins[at : at + TILE_ROWS].astype(bf16)
            piece_refs[o][t * RIM : (t + 1) * RIM] = dot_tn(to_rim, given).astype(bf16)


def put_base(g_ref, upstream, base_ref):
    for t in range(SLOTS):
        center = g_ref[t, 3:19, 3:19, :].reshape(CELLS, C).astype(bf16).astype(f32)
        base_ref[t] = upstream[t * CELLS : (t + 1) * CELLS] + center


def combined(base_ref, pieces, fixed):
    to_cell = fixed[AT_OUT:AT_END, :]
    out = []
    for t in range(SLOTS):
        total = sum(p[t * RIM : (t + 1) * RIM].astype(f32) for p in pieces)
        high = total.astype(bf16)
        low = (total - high.astype(f32)).astype(bf16)
        out.append((base_ref[t] + (dot_tn(to_cell, high) + dot_tn(to_cell, low))).astype(bf16))
    return out


def first_kernel(start, own, m2, m1, p1, p2, fixed, mask, k, small, w_in, w_out,
                 out, rims, pad_b, conv, canon, pad):
    canon[BINS - BLOCK :] = jnp.zeros((BLOCK, C), bf16)
    for o, ref in enumerate((m2, m1, own, p1, p2)):
        for t in range(SLOTS):
            at = (o * SLOTS + t) * TILE_ROWS
            canon[at : at + TILE_ROWS] = dot(fixed[AT_CELL:AT_RIM, :], ref[t, 0:CELLS]).astype(bf16)
    for t in range(SLOTS):
        assemble(pad, t, dot(fixed[AT_PUT:AT_TAKE, :], picked(start, canon, t)), own[t, 0:CELLS])
    pad_b[...] = pad[...].astype(bf16)
    depthwise(pad, k, 0, small[0, 0:1], conv)
    unit, inverse, normed = normalise(conv[...], small[0, 1:2], small[0, 2:3])
    branch = None
    for at in range(0, F, FC):
        pre = dot(normed, w_in[0, 0:C, at : at + FC]) + bias_in(small, 0, at)
        act = (0.5 * pre * (1.0 + lax.erf(pre * ROOT_HALF))).astype(bf16)
        part = dot(act, w_out[0, at : at + FC, :])
        branch = part if branch is None else branch + part
    branch = branch + small[0, 3:4]
    for t in range(SLOTS):
        lo, hi = t * CELLS, (t + 1) * CELLS
        value = (own[t, 0:CELLS].astype(f32) + mask[lo:hi] * branch[lo:hi]).astype(bf16)
        out[t] = value
        rims[t * RIM : (t + 1) * RIM] = dot(fixed[AT_OUT:AT_END, :], value).astype(bf16)


def middle_kernel(start, own, r_own, m2, m1, p1, p2, fixed, cot, mask, k, small, w_in, w_out,
                  q0, q1, q2, q3, q4, base, pad, gc, unit_out, normed_out, g_branch_out, act, g_pre, g_bias, g_normed,
                  canon, conv, g, ring_b, bins):
    canon[BINS - BLOCK :] = jnp.zeros((BLOCK, C), bf16)
    for o, ref in enumerate((m2, m1, r_own, p1, p2)):
        for t in range(SLOTS):
            at = (o * SLOTS + t) * TILE_ROWS
            tile = ref[t * RIM : (t + 1) * RIM]
            canon[at : at + TILE_ROWS] = dot(fixed[AT_RIM:AT_PUT, 0:RIM], tile).astype(bf16)
    for t in range(SLOTS):
        assemble(pad, t, dot(fixed[AT_PUT:AT_TAKE, :], picked(start, canon, t)), own[t])
    depthwise(pad, k, 1, small[1, 0:1], conv)
    unit, inverse, normed = normalise(conv[...], small[1, 1:2], small[1, 2:3])
    upstream = cot[...].reshape(SLOTS * CELLS, C)
    g_branch = upstream * mask[...].astype(bf16)
    unit_out[...] = unit
    normed_out[...] = normed
    g_branch_out[...] = g_branch
    g_conv = pointwise_back(
        1, unit, inverse, normed, g_branch, (small, w_in, w_out), (act, g_pre, g_bias, g_normed)
    )
    spread(g_conv, gc, k, 1, g)
    ring_out(g, ring_b)
    put_pieces(start, fixed, ring_b, bins, (q0, q1, q2, q3, q4))
    put_base(g, upstream.astype(f32), base)


def middle_rest_kernel(own, pad, gc, unit, normed, g_branch, act, g_pre, g_bias, g_normed, mask, small, w_out,
                       out, grads):
    branch = dot(act[...], w_out[1, 0:F]) + small[1, 3:4]
    for t in range(SLOTS):
        lo, hi = t * CELLS, (t + 1) * CELLS
        out[t] = (own[t].astype(f32) + mask[lo:hi] * branch[lo:hi]).astype(bf16)
    weight_terms(pad, gc, unit[...], normed[...], g_branch[...], (act, g_pre, g_bias, g_normed), grads)


def last_kernel(start, base_in, i0, i1, i2, i3, i4, fixed, conv, mask, k, small, w_in, w_out,
                q0, q1, q2, q3, q4, base, gc, unit_out, normed_out, g_branch_out, act, g_pre, g_bias, g_normed,
                g, ring_b, bins):
    parts = combined(base_in, [r[...] for r in (i0, i1, i2, i3, i4)], fixed)
    upstream = jnp.concatenate(parts, axis=0)
    g_branch = upstream * mask[...].astype(bf16)
    unit, inverse, normed = normalise(conv[...], small[0, 1:2], small[0, 2:3])
    unit_out[...] = unit
    normed_out[...] = normed
    g_branch_out[...] = g_branch
    g_conv = pointwise_back(
        0, unit, inverse, normed, g_branch, (small, w_in, w_out), (act, g_pre, g_bias, g_normed)
    )
    spread(g_conv, gc, k, 0, g)
    ring_out(g, ring_b)
    put_pieces(start, fixed, ring_b, bins, (q0, q1, q2, q3, q4))
    put_base(g, upstream.astype(f32), base)


def last_rest_kernel(pad_b, gc, unit, normed, g_branch, act, g_pre, g_bias, g_normed, grads1, packed, pad):
    pad[...] = pad_b[...].astype(f32)
    packed[GROWS:] = grads1[...]
    weight_terms(pad, gc, unit[...], normed[...], g_branch[...], (act, g_pre, g_bias, g_normed), packed)


def closing_kernel(base_in, i0, i1, i2, i3, i4, fixed, out):
    parts = combined(base_in, [r[...] for r in (i0, i1, i2, i3, i4)], fixed)
    for t in range(SLOTS):
        out[t] = parts[t]


def unpack_kernel(scale, packed, dw, dwb, gain, shift, w_in, b_in, w_out, b_out):
    for b in range(BLOCKS):
        at = b * GROWS
        value = packed[at : at + GROWS].astype(f32) * scale
        for c0 in range(0, F, C):
            w_in[b, :, c0 : c0 + C] = value[c0 : c0 + C]
            row = SMALL + 52 + c0 // C
            b_in[b : b + 1, c0 : c0 + C] = value[row : row + 1]
        w_out[b] = value[512:1024]
        dw[b] = value[SMALL : SMALL + 49]
        dwb[b : b + 1] = value[SMALL + 49 : SMALL + 50]
        gain[b : b + 1] = value[SMALL + 50 : SMALL + 51]
        shift[b : b + 1] = value[SMALL + 51 : SMALL + 52]
        b_out[b : b + 1] = value[SMALL + 56 : SMALL + 57]


def shape(dims, kind):
    return jax.ShapeDtypeStruct(dims, kind)


def call(kernel, outs, args, scratch=(), scalars=0, flops=1000000, name=None):
    vmem = pl.BlockSpec(memory_space=pltpu.VMEM)
    size = sum(math.prod(a.shape) * a.dtype.itemsize for a in list(args) + list(outs))
    return pl.pallas_call(
        kernel,
        out_shape=outs,
        in_specs=[pl.BlockSpec(memory_space=pltpu.SMEM)] * scalars + [vmem] * (len(args) - scalars),
        out_specs=[vmem] * len(outs),
        scratch_shapes=list(scratch),
        compiler_params=pltpu.CompilerParams(vmem_limit_bytes=VMEM),
        cost_estimate=pl.CostEstimate(flops=flops, bytes_accessed=size, transcendentals=0),
        name=name,
    )(*args)


def shift_by(x, by):
    n = lax.axis_size("space")
    return lax.ppermute(x, "space", [(i, (i + by) % n) for i in range(n)])


def strides(axis):
    return {"core": (1, 2), "z": (2, 4), "x": (8, 4), "y": (32, 4)}[axis]


def coordinate(axis):
    stride, extent = strides(axis)
    return (lax.axis_index("space") // stride) % extent


def along(x, axis, move):
    if axis == "dp":
        return lax.ppermute(x, "dp", [(0, 1), (1, 0)])
    stride, extent = strides(axis)
    pairs = []
    for i in range(lax.axis_size("space")):
        c = (i // stride) % extent
        pairs.append((i, i + (move(c) - c) * stride))
    return lax.ppermute(x, "space", pairs)


def scatter_sum(x, axis, kind):
    extent = strides(axis)[1]
    me = coordinate(axis)
    parts = x.reshape((extent, -1, C))
    total = lax.dynamic_index_in_dim(parts, me, 0, keepdims=False)
    for d in range(1, extent):
        piece = lax.dynamic_index_in_dim(parts, (me + d) % extent, 0, keepdims=False).astype(kind)
        total = total + along(piece, axis, lambda c: (c + d) % extent).astype(f32)
    return total


def exchange_sum(x, axis, mask):
    return x + along(x, axis, lambda c: c ^ mask)


def collect(x, axis):
    extent = strides(axis)[1]
    me = coordinate(axis)
    out = lax.dynamic_update_index_in_dim(jnp.zeros((extent,) + x.shape, x.dtype), x, me, 0)
    for d in range(1, extent):
        got = along(x, axis, lambda c: (c + d) % extent)
        out = lax.dynamic_update_index_in_dim(out, got, (me - d) % extent, 0)
    return out.reshape(-1, C)


def reduced(g, beside):
    x = scatter_sum(g, "core", f32)
    x = scatter_sum(x, "x", bf16)
    x, *beside = lax.optimization_barrier((x, *beside))
    x = scatter_sum(x, "y", bf16)
    x = exchange_sum(x, "z", 1)
    x = exchange_sum(x, "z", 2)
    x = exchange_sum(x, "dp", 1)
    x = x.astype(bf16)
    x = collect(x, "y")
    x = collect(x, "x")
    return collect(x, "core"), beside


def piece_starts(neighbors, codes):
    n = lax.axis_size("space")
    distance = jnp.mod(jnp.floor_divide(neighbors, SLOTS) - lax.axis_index("space"), n)
    distance = jnp.where(distance > n // 2, distance - n, distance)
    begin = ((distance + RANGE) * SLOTS + jnp.mod(neighbors, SLOTS)) * TILE_ROWS + codes * BLOCK
    return jnp.where(neighbors >= 0, begin, BINS - BLOCK).astype(jnp.int32)


def local(fields, cotangent, ocean_mask, neighbors, codes, dw_kernel, dw_bias, ln_gain, ln_bias, w_in, b_in, w_out,
          b_out):
    dims = fields.shape
    own = fields.reshape(SLOTS, CELLS, C)
    raw = [shift_by(own, -o) for o in OFFSETS]
    start = piece_starts(neighbors, codes)
    fixed = (jnp.asarray(fixed_rows())[:, None] == jnp.arange(CELLS, dtype=jnp.int32)[None, :]).astype(bf16)
    mask = ocean_mask.astype(f32).reshape(SLOTS * CELLS, 1)
    rows = [p.reshape(BLOCKS, 1, C) for p in (dw_bias, ln_gain, ln_bias, b_out)]
    small = jnp.concatenate(rows + [b_in.reshape(BLOCKS, F // C, C)], axis=1)
    w_in = jnp.pad(w_in, ((0, 0), (0, 16), (0, 0)))
    w_out = jnp.pad(w_out, ((0, 0), (0, 16), (0, 0)))
    center = jnp.pad(own, ((0, 0), (0, 16), (0, 0)))
    start, fixed, mask, small, w_in, w_out, center = lax.optimization_barrier(
        (start, fixed, mask, small, w_in, w_out, center)
    )
    tile = (SLOTS, CELLS, C)
    flat = (SLOTS * CELLS, C)
    wide = (SLOTS * CELLS, F)
    padded = (SLOTS, 22, 32, C)
    rims_shape = shape((SLOTS * RIM, C), bf16)
    out0, rims, pad0, conv0 = call(
        first_kernel,
        [shape(tile, bf16), rims_shape, shape(padded, bf16), shape(flat, f32)],
        [start, center, *raw, fixed, mask, dw_kernel, small, w_in, w_out],
        [pltpu.VMEM((BINS, C), bf16), pltpu.VMEM(padded, f32)],
        scalars=1, flops=2000000000, name="block0_forward",
    )
    got = [shift_by(rims, -o) for o in OFFSETS]
    back = [
        pltpu.VMEM((SLOTS, 22, 24, C), f32), pltpu.VMEM((SLOTS * RING_T, C), bf16), pltpu.VMEM((BINS, C), f32)
    ]
    kept = [
        shape((SLOTS, TS, 32, C), f32), shape(flat, f32), shape(flat, bf16), shape(flat, bf16),
        shape(wide, bf16), shape(wide, bf16), shape((1, F), f32), shape(flat, f32),
    ]
    q0, q1, q2, q3, q4, base1, pad1, *saved = call(
        middle_kernel,
        [rims_shape] * 5 + [shape(tile, f32), shape(padded, f32)] + kept,
        [start, out0, rims, *got, fixed, cotangent.reshape(tile), mask, dw_kernel, small, w_in, w_out],
        [pltpu.VMEM((BINS, C), bf16), pltpu.VMEM(flat, f32)] + back,
        scalars=1, flops=4000000000, name="block1_both",
    )
    pieces = [q2] + [shift_by(q, o) for q, o in zip((q0, q1, q3, q4), OFFSETS)]
    out1, grads1 = call(
        middle_rest_kernel,
        [shape(tile, bf16), shape((GROWS, C), f32)],
        [out0, pad1, *saved, mask, small, w_out],
        flops=4000000000, name="block1_rest",
    )
    q0, q1, q2, q3, q4, base0, *saved = call(
        last_kernel,
        [rims_shape] * 5 + [shape(tile, f32)] + kept,
        [start, base1, *pieces, fixed, conv0, mask, dw_kernel, small, w_in, w_out],
        back,
        scalars=1, flops=3000000000, name="block0_backward",
    )
    pieces = [q2] + [shift_by(q, o) for q, o in zip((q0, q1, q3, q4), OFFSETS)]
    (packed,) = call(
        last_rest_kernel,
        [shape((BLOCKS * GROWS, C), f32)],
        [pad0, *saved, grads1],
        [pltpu.VMEM(padded, f32)],
        flops=4000000000, name="block0_rest",
    )
    packed, pieces = reduced(packed, pieces)
    (field_grad,) = call(
        closing_kernel, [shape(tile, bf16)], [base0, *pieces, fixed], flops=100000000, name="closing"
    )
    scale = 1.0 / math.sqrt(SLOTS * CELLS * lax.axis_size("dp") * lax.axis_size("space"))
    grads = call(
        lambda *refs: unpack_kernel(scale, *refs),
        [
            shape((BLOCKS, 49, C), f32), shape((BLOCKS, C), f32), shape((BLOCKS, C), f32), shape((BLOCKS, C), f32),
            shape((BLOCKS, C, F), f32), shape((BLOCKS, F), f32), shape((BLOCKS, F, C), f32), shape((BLOCKS, C), f32),
        ],
        [packed], flops=1000000, name="unpack",
    )
    return (out1.reshape(dims), field_grad.reshape(dims), *grads)


def solution(mesh):
    placed = (
        P("dp", "space", None, None, None),
        P("dp", "space", None, None, None),
        P("space", None, None),
        P("space", None),
        P("space", None),
    ) + (P(),) * 8
    return jax.shard_map(
        local,
        mesh=mesh,
        in_specs=placed,
        out_specs=(P("dp", "space", None, None, None), P("dp", "space", None, None, None)) + (P(),) * 8,
        check_vma=False,
    )
```

```python
import math

import jax
import jax.numpy as jnp
import numpy as np
from jax import lax
from jax.experimental import pallas as pl
from jax.experimental.pallas import tpu as pltpu
from jax.sharding import PartitionSpec as P

RANGE = 2
BLOCKS = 2
WINDOW = 2 * RANGE + 1
OFFSETS = (-2, -1, 1, 2)
RETURNS = (2, 1, -1, -2)

EPS = 1e-06
ROOT_HALF = 0.7071067811865476
INV_ROOT_TAU = 0.3989422804014327

TS = 16
CELLS = TS * TS
C = 128
F = 512
FC = 256
SLOTS = 2
RIM = 160
RING_S = 320
RING_T = 272
BLOCK = 64
TILE_ROWS = 4 * BLOCK
BINS = WINDOW * SLOTS * TILE_ROWS + BLOCK
AT_CELL, AT_RIM, AT_PUT, AT_TAKE, AT_OUT, AT_END = 0, 256, 512, 832, 1104, 1264
GROWS = 1152
SMALL = 1024
VMEM = 14 * 1024 * 1024

f32 = jnp.float32
bf16 = jnp.bfloat16


def rim_of_cell():
    rim = np.full((TS, TS), -1, np.int32)
    for i in range(TS):
        for j in range(TS):
            if i < 3:
                rim[i, j] = i * TS + j
            elif i >= 13:
                rim[i, j] = 48 + (i - 13) * TS + j
            elif j < 3:
                rim[i, j] = 96 + (i - 3) * 6 + j
            elif j >= 13:
                rim[i, j] = 96 + (i - 3) * 6 + 3 + (j - 13)
    return rim


def pieces_of(code):
    turned = np.rot90(np.arange(CELLS).reshape(TS, TS), code)
    out = np.full((BLOCK,), -1, np.int32)
    out[0:48] = turned[0:3][::-1, ::-1].reshape(-1)
    out[48:57] = turned[0:3, 0:3][::-1, ::-1].reshape(-1)
    return out


def frame_positions():
    frame = np.arange(22 * 22).reshape(22, 22)
    row = np.full((22 * 22,), -1, np.int32)
    for q in range(4):
        turned = np.rot90(frame, q)
        row[turned[0:3, 3:19].reshape(-1)] = q * 48 + np.arange(48)
        row[turned[0:3, 0:3].reshape(-1)] = 192 + q * 16 + np.arange(9)
    return row.reshape(22, 22)


def order_s():
    out = []
    for rows in (range(0, 3), range(19, 22)):
        for p in rows:
            out += [(p, cc - 5) if 0 <= cc - 5 < 22 else None for cc in range(32)]
    for p in range(3, 19):
        out += [(p, 19), (p, 20), (p, 21), None, None, (p, 0), (p, 1), (p, 2)]
    return out


def order_t():
    out = []
    for rows in (range(0, 3), range(19, 22)):
        for p in rows:
            out += [(p, cc) if cc < 22 else None for cc in range(24)]
    for p in range(3, 19):
        out += [(p, 0), (p, 1), (p, 2), (p, 19), (p, 20), (p, 21), None, None]
    return out


def fixed_rows():
    rim = rim_of_cell().reshape(-1)
    cell_of_rim = np.full((RIM,), -1, np.int32)
    for cell in range(CELLS):
        if rim[cell] >= 0:
            cell_of_rim[rim[cell]] = cell
    codes = np.concatenate([pieces_of(code) for code in range(4)])
    from_rim = np.where(codes >= 0, rim[codes], -1)
    at = frame_positions()
    put = np.array([-1 if p is None else at[p] for p in order_s()], np.int32)
    take = np.array([-1 if p is None else at[p] for p in order_t()], np.int32)
    return np.concatenate([codes, from_rim, put, take, cell_of_rim]).astype(np.int32)


def dot(a, b):
    return lax.dot_general(a, b, (((1,), (0,)), ((), ())), preferred_element_type=f32)


def dot_nt(a, b):
    return lax.dot_general(a, b, (((1,), (1,)), ((), ())), preferred_element_type=f32)


def dot_tn(a, b):
    return lax.dot_general(a, b, (((0,), (0,)), ((), ())), preferred_element_type=f32)


def assemble(pad_ref, t, ring, center):
    pad_ref[t, 0:3] = ring[0:96].reshape(3, 32, C)
    pad_ref[t, 19:22] = ring[96:192].reshape(3, 32, C)
    sides = ring[192:320].reshape(TS, 8, C)
    pad_ref[t, 3:19, 0:8] = sides
    pad_ref[t, 3:19, 24:32] = sides
    pad_ref[t, 3:19, 8:24] = center.astype(f32).reshape(TS, TS, C)


def depthwise(pad_ref, k_ref, b, bias, conv_ref):
    for t in range(SLOTS):
        for half in range(2):
            total = jnp.broadcast_to(bias.reshape(1, 1, C), (8, TS, C))
            for e in range(7):
                moved = pad_ref[t, 8 * half : 8 * half + 14, 5 + e : 21 + e, :]
                for a in range(7):
                    tap = k_ref[b, 7 * a + e : 7 * a + e + 1, :].reshape(1, 1, C)
                    total = total + tap * moved[a : a + 8]
            at = t * CELLS + half * 128
            conv_ref[at : at + 128] = total.reshape(128, C)


def normalise(conv, gain, shift):
    centred = conv - jnp.mean(conv, axis=-1, keepdims=True)
    inverse = lax.rsqrt(jnp.mean(centred * centred, axis=-1, keepdims=True) + EPS)
    unit = centred * inverse
    return unit, inverse, (unit * gain + shift).astype(bf16)


def spread(g_conv, gc_ref, k_ref, b, g_ref):
    for t in range(SLOTS):
        gc_ref[t, :, 0:8] = jnp.zeros((TS, 8, C), f32)
        gc_ref[t, :, 24:32] = jnp.zeros((TS, 8, C), f32)
        gc_ref[t, :, 8:24] = g_conv[t * CELLS : (t + 1) * CELLS].reshape(TS, TS, C)
    for t in range(SLOTS):
        for first, last in ((0, 6), (6, 11), (11, 16), (16, 22)):
            totals = [None] * (last - first)
            low, high = max(0, first - 6), min(TS, last)
            for e in range(7):
                moved = gc_ref[t, low:high, 8 - e : 32 - e, :]
                for a in range(7):
                    tap = k_ref[b, 7 * a + e : 7 * a + e + 1, :]
                    for p in range(first, last):
                        r = p - a
                        if 0 <= r < TS:
                            term = tap * moved[r - low]
                            was = totals[p - first]
                            totals[p - first] = term if was is None else was + term
            for p in range(first, last):
                g_ref[t, p] = totals[p - first]


def ring_out(g_ref, ring_ref):
    for t in range(SLOTS):
        at = t * RING_T
        ring_ref[at : at + 72] = g_ref[t, 0:3].reshape(72, C).astype(bf16)
        ring_ref[at + 72 : at + 144] = g_ref[t, 19:22].reshape(72, C).astype(bf16)
        left = g_ref[t, 3:19, 0:8]
        right = g_ref[t, 3:19, 16:24]
        column = lax.broadcasted_iota(jnp.int32, (TS, 8, C), 1)
        ring_ref[at + 144 : at + 272] = jnp.where(column < 3, left, right).reshape(128, C).astype(bf16)


def kernel_terms(pad_ref, gc_ref, grads_ref):
    for e in range(7):
        sums = [None] * 7
        for t in range(SLOTS):
            for half in range(2):
                moved = pad_ref[t, 8 * half : 8 * half + 14, 5 + e : 21 + e, :]
                here = gc_ref[t, 8 * half : 8 * half + 8, 8:24]
                for a in range(7):
                    part = jnp.sum(here * moved[a : a + 8], axis=0)
                    part = part[0:8] + part[8:16]
                    sums[a] = part if sums[a] is None else sums[a] + part
        for a in range(7):
            at = SMALL + 7 * a + e
            grads_ref[at : at + 1] = jnp.sum(sums[a], axis=0, keepdims=True)


def column_sum(x):
    return jnp.sum(x, axis=0, keepdims=True)


def bias_in(small_ref, b, at):
    first = 4 + at // C
    return jnp.concatenate([small_ref[b, r : r + 1] for r in range(first, first + FC // C)], axis=1)


def pointwise_back(b, unit, inverse, normed, g_branch, wts, kept):
    small_ref, w_in_ref, w_out_ref = wts
    act_ref, g_pre_ref, g_bias_ref, g_normed_ref = kept
    g_normed = None
    for at in range(0, F, FC):
        w1 = w_in_ref[b, 0:C, at : at + FC]
        w2 = w_out_ref[b, at : at + FC, :]
        pre = dot(normed, w1) + bias_in(small_ref, b, at)
        half = 0.5 * (1.0 + lax.erf(pre * ROOT_HALF))
        act_ref[:, at : at + FC] = (pre * half).astype(bf16)
        slope = half + pre * INV_ROOT_TAU * jnp.exp(-0.5 * pre * pre)
        g_pre = dot_nt(g_branch, w2) * slope
        g_bias_ref[0:1, at : at + FC] = column_sum(g_pre)
        g_pre_b = g_pre.astype(bf16)
        g_pre_ref[:, at : at + FC] = g_pre_b
        part = dot_nt(g_pre_b, w1)
        g_normed = part if g_normed is None else g_normed + part
    g_normed_ref[...] = g_normed
    g_unit = g_normed * small_ref[b, 1:2]
    return inverse * (
        g_unit
        - jnp.mean(g_unit, axis=-1, keepdims=True)
        - unit * jnp.mean(g_unit * unit, axis=-1, keepdims=True)
    )


def weight_terms(pad_ref, gc_ref, unit, normed, g_branch, kept, grads_ref):
    act_ref, g_pre_ref, g_bias_ref, g_normed_ref = kept
    grads_ref[SMALL + 49 : GROWS] = jnp.zeros((GROWS - SMALL - 49, C), f32)
    for at in range(0, F, FC):
        g_w1 = dot_tn(normed, g_pre_ref[:, at : at + FC])
        for c0 in range(0, FC, C):
            grads_ref[at + c0 : at + c0 + C] = g_w1[:, c0 : c0 + C]
            row = SMALL + 52 + (at + c0) // C
            grads_ref[row : row + 1] = g_bias_ref[0:1, at + c0 : at + c0 + C]
        grads_ref[512 + at : 512 + at + FC] = dot_tn(act_ref[:, at : at + FC], g_branch)
    g_normed = g_normed_ref[...]
    g_conv_sum = sum(jnp.sum(gc_ref[t, :, 8:24].reshape(CELLS, C), axis=0, keepdims=True) for t in range(SLOTS))
    grads_ref[SMALL + 49 : SMALL + 50] = g_conv_sum
    grads_ref[SMALL + 50 : SMALL + 51] = column_sum(g_normed * unit)
    grads_ref[SMALL + 51 : SMALL + 52] = column_sum(g_normed)
    grads_ref[SMALL + 56 : SMALL + 57] = column_sum(g_branch.astype(f32))
    kernel_terms(pad_ref, gc_ref, grads_ref)


def picked(start, canon, t):
    parts = []
    for q in range(8):
        first = pl.multiple_of(start[t, q], BLOCK)
        parts.append(canon[pl.ds(first, 48), :] if q < 4 else canon[pl.ds(first + 48, 16), :])
    return jnp.concatenate(parts, axis=0)


def put_pieces(start, fixed, ring_ref, bins, piece_refs):
    bins[...] = jnp.zeros((BINS, C), f32)
    for t in range(SLOTS):
        ring = ring_ref[t * RING_T : (t + 1) * RING_T]
        parts = dot_tn(fixed[AT_TAKE:AT_OUT, :], ring)
        for q in range(8):
            first = pl.multiple_of(start[t, q], BLOCK)
            if q < 4:
                bins[pl.ds(first, 48), :] += parts[q * 48 : (q + 1) * 48]
            else:
                bins[pl.ds(first + 48, 16), :] += parts[192 + (q - 4) * 16 : 208 + (q - 4) * 16]
    to_rim = fixed[AT_RIM:AT_PUT, 0:RIM]
    for o in range(WINDOW):
        for t in range(SLOTS):
            at = (o * SLOTS + t) * TILE_ROWS
            given = bins[at : at + TILE_ROWS].astype(bf16)
            piece_refs[o][t * RIM : (t + 1) * RIM] = dot_tn(to_rim, given).astype(bf16)


def put_base(g_ref, upstream, base_ref):
    for t in range(SLOTS):
        center = g_ref[t, 3:19, 3:19, :].reshape(CELLS, C).astype(bf16).astype(f32)
        base_ref[t] = upstream[t * CELLS : (t + 1) * CELLS] + center


def combined(base_ref, pieces, fixed):
    to_cell = fixed[AT_OUT:AT_END, :]
    out = []
    for t in range(SLOTS):
        total = sum(p[t * RIM : (t + 1) * RIM].astype(f32) for p in pieces)
        high = total.astype(bf16)
        low = (total - high.astype(f32)).astype(bf16)
        out.append((base_ref[t] + (dot_tn(to_cell, high) + dot_tn(to_cell, low))).astype(bf16))
    return out


def first_kernel(start, own, m2, m1, p1, p2, fixed, mask, k, small, w_in, w_out,
                 out, rims, pad_b, conv, canon, pad):
    canon[BINS - BLOCK :] = jnp.zeros((BLOCK, C), bf16)
    for o, ref in enumerate((m2, m1, own, p1, p2)):
        for t in range(SLOTS):
            at = (o * SLOTS + t) * TILE_ROWS
            canon[at : at + TILE_ROWS] = dot(fixed[AT_CELL:AT_RIM, :], ref[t, 0:CELLS]).astype(bf16)
    for t in range(SLOTS):
        assemble(pad, t, dot(fixed[AT_PUT:AT_TAKE, :], picked(start, canon, t)), own[t, 0:CELLS])
    pad_b[...] = pad[...].astype(bf16)
    depthwise(pad, k, 0, small[0, 0:1], conv)
    unit, inverse, normed = normalise(conv[...], small[0, 1:2], small[0, 2:3])
    branch = None
    for at in range(0, F, FC):
        pre = dot(normed, w_in[0, 0:C, at : at + FC]) + bias_in(small, 0, at)
        act = (0.5 * pre * (1.0 + lax.erf(pre * ROOT_HALF))).astype(bf16)
        part = dot(act, w_out[0, at : at + FC, :])
        branch = part if branch is None else branch + part
    branch = branch + small[0, 3:4]
    for t in range(SLOTS):
        lo, hi = t * CELLS, (t + 1) * CELLS
        value = (own[t, 0:CELLS].astype(f32) + mask[lo:hi] * branch[lo:hi]).astype(bf16)
        out[t] = value
        rims[t * RIM : (t + 1) * RIM] = dot(fixed[AT_OUT:AT_END, :], value).astype(bf16)


def middle_kernel(start, own, r_own, m2, m1, p1, p2, fixed, cot, mask, k, small, w_in, w_out,
                  q0, q1, q2, q3, q4, base, pad, gc, unit_out, normed_out, g_branch_out, act, g_pre, g_bias, g_normed,
                  canon, conv, g, ring_b, bins):
    canon[BINS - BLOCK :] = jnp.zeros((BLOCK, C), bf16)
    for o, ref in enumerate((m2, m1, r_own, p1, p2)):
        for t in range(SLOTS):
            at = (o * SLOTS + t) * TILE_ROWS
            tile = ref[t * RIM : (t + 1) * RIM]
            canon[at : at + TILE_ROWS] = dot(fixed[AT_RIM:AT_PUT, 0:RIM], tile).astype(bf16)
    for t in range(SLOTS):
        assemble(pad, t, dot(fixed[AT_PUT:AT_TAKE, :], picked(start, canon, t)), own[t])
    depthwise(pad, k, 1, small[1, 0:1], conv)
    unit, inverse, normed = normalise(conv[...], small[1, 1:2], small[1, 2:3])
    upstream = cot[...].reshape(SLOTS * CELLS, C)
    g_branch = upstream * mask[...].astype(bf16)
    unit_out[...] = unit
    normed_out[...] = normed
    g_branch_out[...] = g_branch
    g_conv = pointwise_back(
        1, unit, inverse, normed, g_branch, (small, w_in, w_out), (act, g_pre, g_bias, g_normed)
    )
    spread(g_conv, gc, k, 1, g)
    ring_out(g, ring_b)
    put_pieces(start, fixed, ring_b, bins, (q0, q1, q2, q3, q4))
    put_base(g, upstream.astype(f32), base)


def middle_rest_kernel(own, pad, gc, unit, normed, g_branch, act, g_pre, g_bias, g_normed, mask, small, w_out,
                       out, grads):
    branch = dot(act[...], w_out[1, 0:F]) + small[1, 3:4]
    for t in range(SLOTS):
        lo, hi = t * CELLS, (t + 1) * CELLS
        out[t] = (own[t].astype(f32) + mask[lo:hi] * branch[lo:hi]).astype(bf16)
    weight_terms(pad, gc, unit[...], normed[...], g_branch[...], (act, g_pre, g_bias, g_normed), grads)


def last_kernel(start, base_in, i0, i1, i2, i3, i4, fixed, conv, mask, k, small, w_in, w_out,
                q0, q1, q2, q3, q4, base, gc, unit_out, normed_out, g_branch_out, act, g_pre, g_bias, g_normed,
                g, ring_b, bins):
    parts = combined(base_in, [r[...] for r in (i0, i1, i2, i3, i4)], fixed)
    upstream = jnp.concatenate(parts, axis=0)
    g_branch = upstream * mask[...].astype(bf16)
    unit, inverse, normed = normalise(conv[...], small[0, 1:2], small[0, 2:3])
    unit_out[...] = unit
    normed_out[...] = normed
    g_branch_out[...] = g_branch
    g_conv = pointwise_back(
        0, unit, inverse, normed, g_branch, (small, w_in, w_out), (act, g_pre, g_bias, g_normed)
    )
    spread(g_conv, gc, k, 0, g)
    ring_out(g, ring_b)
    put_pieces(start, fixed, ring_b, bins, (q0, q1, q2, q3, q4))
    put_base(g, upstream.astype(f32), base)


def last_rest_kernel(pad_b, gc, unit, normed, g_branch, act, g_pre, g_bias, g_normed, grads1, packed, pad):
    pad[...] = pad_b[...].astype(f32)
    packed[GROWS:] = grads1[...]
    weight_terms(pad, gc, unit[...], normed[...], g_branch[...], (act, g_pre, g_bias, g_normed), packed)


def closing_kernel(base_in, i0, i1, i2, i3, i4, fixed, out):
    parts = combined(base_in, [r[...] for r in (i0, i1, i2, i3, i4)], fixed)
    for t in range(SLOTS):
        out[t] = parts[t]


def unpack_kernel(scale, packed, dw, dwb, gain, shift, w_in, b_in, w_out, b_out):
    for b in range(BLOCKS):
        at = b * GROWS
        value = packed[at : at + GROWS].astype(f32) * scale
        for c0 in range(0, F, C):
            w_in[b, :, c0 : c0 + C] = value[c0 : c0 + C]
            row = SMALL + 52 + c0 // C
            b_in[b : b + 1, c0 : c0 + C] = value[row : row + 1]
        w_out[b] = value[512:1024]
        dw[b] = value[SMALL : SMALL + 49]
        dwb[b : b + 1] = value[SMALL + 49 : SMALL + 50]
        gain[b : b + 1] = value[SMALL + 50 : SMALL + 51]
        shift[b : b + 1] = value[SMALL + 51 : SMALL + 52]
        b_out[b : b + 1] = value[SMALL + 56 : SMALL + 57]


def shape(dims, kind):
    return jax.ShapeDtypeStruct(dims, kind)


def call(kernel, outs, args, scratch=(), scalars=0, flops=1000000, name=None):
    vmem = pl.BlockSpec(memory_space=pltpu.VMEM)
    size = sum(math.prod(a.shape) * a.dtype.itemsize for a in list(args) + list(outs))
    return pl.pallas_call(
        kernel,
        out_shape=outs,
        in_specs=[pl.BlockSpec(memory_space=pltpu.SMEM)] * scalars + [vmem] * (len(args) - scalars),
        out_specs=[vmem] * len(outs),
        scratch_shapes=list(scratch),
        compiler_params=pltpu.CompilerParams(vmem_limit_bytes=VMEM),
        cost_estimate=pl.CostEstimate(flops=flops, bytes_accessed=size, transcendentals=0),
        name=name,
    )(*args)


def shift_by(x, by):
    n = lax.axis_size("space")
    return lax.ppermute(x, "space", [(i, (i + by) % n) for i in range(n)])


def strides(axis):
    return {"core": (1, 2), "z": (2, 4), "x": (8, 4), "y": (32, 4)}[axis]


def coordinate(axis):
    stride, extent = strides(axis)
    return (lax.axis_index("space") // stride) % extent


def along(x, axis, move):
    stride, extent = strides(axis)
    pairs = []
    for i in range(lax.axis_size("space")):
        c = (i // stride) % extent
        pairs.append((i, i + (move(c) - c) * stride))
    return lax.ppermute(x, "space", pairs)


def scatter_sum(x, axis, kind):
    extent = strides(axis)[1]
    me = coordinate(axis)
    parts = x.reshape((extent, -1, C))
    total = lax.dynamic_index_in_dim(parts, me, 0, keepdims=False)
    for d in range(1, extent):
        piece = lax.dynamic_index_in_dim(parts, (me + d) % extent, 0, keepdims=False).astype(kind)
        total = total + along(piece, axis, lambda c: (c + d) % extent).astype(f32)
    return total


def exchange_sum(x, axis, mask):
    return x + along(x, axis, lambda c: c ^ mask)


def collect(x, axis):
    extent = strides(axis)[1]
    me = coordinate(axis)
    out = lax.dynamic_update_index_in_dim(jnp.zeros((extent,) + x.shape, x.dtype), x, me, 0)
    for d in range(1, extent):
        got = along(x, axis, lambda c: (c + d) % extent)
        out = lax.dynamic_update_index_in_dim(out, got, (me - d) % extent, 0)
    return out.reshape(-1, C)


def across(x):
    n = lax.axis_size("space")
    pairs = []
    for i in range(2 * n):
        stride, extent = strides("z")
        half, s = i // n, i % n
        z = (s // stride) % extent
        pairs.append((i, (1 - half) * n + s + ((z ^ 2) - z) * stride))
    return x + lax.ppermute(x, ("dp", "space"), pairs)


def reduced(g, beside):
    x = scatter_sum(g, "core", f32)
    x, *beside = lax.optimization_barrier((x, *beside))
    x = scatter_sum(x, "x", bf16)
    x = scatter_sum(x, "y", bf16)
    x = exchange_sum(x, "z", 1)
    x = exchange_sum(x, "z", 2)
    x = across(x)
    x = x.astype(bf16)
    x = collect(x, "y")
    x = collect(x, "x")
    return collect(x, "core"), beside


def piece_starts(neighbors, codes):
    n = lax.axis_size("space")
    distance = jnp.mod(jnp.floor_divide(neighbors, SLOTS) - lax.axis_index("space"), n)
    distance = jnp.where(distance > n // 2, distance - n, distance)
    begin = ((distance + RANGE) * SLOTS + jnp.mod(neighbors, SLOTS)) * TILE_ROWS + codes * BLOCK
    return jnp.where(neighbors >= 0, begin, BINS - BLOCK).astype(jnp.int32)


def local(fields, cotangent, ocean_mask, neighbors, codes, dw_kernel, dw_bias, ln_gain, ln_bias, w_in, b_in, w_out,
          b_out):
    dims = fields.shape
    own = fields.reshape(SLOTS, CELLS, C)
    raw = [shift_by(own, -o) for o in OFFSETS]
    start = piece_starts(neighbors, codes)
    fixed = (jnp.asarray(fixed_rows())[:, None] == jnp.arange(CELLS, dtype=jnp.int32)[None, :]).astype(bf16)
    mask = ocean_mask.astype(f32).reshape(SLOTS * CELLS, 1)
    rows = [p.reshape(BLOCKS, 1, C) for p in (dw_bias, ln_gain, ln_bias, b_out)]
    small = jnp.concatenate(rows + [b_in.reshape(BLOCKS, F // C, C)], axis=1)
    w_in = jnp.pad(w_in, ((0, 0), (0, 16), (0, 0)))
    w_out = jnp.pad(w_out, ((0, 0), (0, 16), (0, 0)))
    center = jnp.pad(own, ((0, 0), (0, 16), (0, 0)))
    start, fixed, mask, small, w_in, w_out, center = lax.optimization_barrier(
        (start, fixed, mask, small, w_in, w_out, center)
    )
    tile = (SLOTS, CELLS, C)
    flat = (SLOTS * CELLS, C)
    wide = (SLOTS * CELLS, F)
    padded = (SLOTS, 22, 32, C)
    rims_shape = shape((SLOTS * RIM, C), bf16)
    out0, rims, pad0, conv0 = call(
        first_kernel,
        [shape(tile, bf16), rims_shape, shape(padded, bf16), shape(flat, f32)],
        [start, center, *raw, fixed, mask, dw_kernel, small, w_in, w_out],
        [pltpu.VMEM((BINS, C), bf16), pltpu.VMEM(padded, f32)],
        scalars=1, flops=2000000000, name="block0_forward",
    )
    got = [shift_by(rims, -o) for o in OFFSETS]
    back = [
        pltpu.VMEM((SLOTS, 22, 24, C), f32), pltpu.VMEM((SLOTS * RING_T, C), bf16), pltpu.VMEM((BINS, C), f32)
    ]
    kept = [
        shape((SLOTS, TS, 32, C), f32), shape(flat, f32), shape(flat, bf16), shape(flat, bf16),
        shape(wide, bf16), shape(wide, bf16), shape((1, F), f32), shape(flat, f32),
    ]
    q0, q1, q2, q3, q4, base1, pad1, *saved = call(
        middle_kernel,
        [rims_shape] * 5 + [shape(tile, f32), shape(padded, f32)] + kept,
        [start, out0, rims, *got, fixed, cotangent.reshape(tile), mask, dw_kernel, small, w_in, w_out],
        [pltpu.VMEM((BINS, C), bf16), pltpu.VMEM(flat, f32)] + back,
        scalars=1, flops=4000000000, name="block1_both",
    )
    pieces = [q2] + [shift_by(q, o) for q, o in zip((q4, q3, q1, q0), RETURNS)]
    out1, grads1 = call(
        middle_rest_kernel,
        [shape(tile, bf16), shape((GROWS, C), f32)],
        [out0, pad1, *saved, mask, small, w_out],
        flops=4000000000, name="block1_rest",
    )
    q0, q1, q2, q3, q4, base0, *saved = call(
        last_kernel,
        [rims_shape] * 5 + [shape(tile, f32)] + kept,
        [start, base1, *pieces, fixed, conv0, mask, dw_kernel, small, w_in, w_out],
        back,
        scalars=1, flops=3000000000, name="block0_backward",
    )
    pieces = [q2] + [shift_by(q, o) for q, o in zip((q4, q3, q1, q0), RETURNS)]
    (packed,) = call(
        last_rest_kernel,
        [shape((BLOCKS * GROWS, C), f32)],
        [pad0, *saved, grads1],
        [pltpu.VMEM(padded, f32)],
        flops=4000000000, name="block0_rest",
    )
    packed, pieces = reduced(packed, pieces)
    (field_grad,) = call(
        closing_kernel, [shape(tile, bf16)], [base0, *pieces, fixed], flops=100000000, name="closing"
    )
    scale = 1.0 / math.sqrt(SLOTS * CELLS * lax.axis_size("dp") * lax.axis_size("space"))
    grads = call(
        lambda *refs: unpack_kernel(scale, *refs),
        [
            shape((BLOCKS, 49, C), f32), shape((BLOCKS, C), f32), shape((BLOCKS, C), f32), shape((BLOCKS, C), f32),
            shape((BLOCKS, C, F), f32), shape((BLOCKS, F), f32), shape((BLOCKS, F, C), f32), shape((BLOCKS, C), f32),
        ],
        [packed], flops=1000000, name="unpack",
    )
    return (out1.reshape(dims), field_grad.reshape(dims), *grads)


def solution(mesh):
    placed = (
        P("dp", "space", None, None, None),
        P("dp", "space", None, None, None),
        P("space", None, None),
        P("space", None),
        P("space", None),
    ) + (P(),) * 8
    return jax.shard_map(
        local,
        mesh=mesh,
        in_specs=placed,
        out_specs=(P("dp", "space", None, None, None), P("dp", "space", None, None, None)) + (P(),) * 8,
        check_vma=False,
    )
```

```python
import math

import jax
import jax.numpy as jnp
import numpy as np
from jax import lax
from jax.experimental import pallas as pl
from jax.experimental.pallas import tpu as pltpu
from jax.sharding import PartitionSpec as P

RANGE = 2
BLOCKS = 2
WINDOW = 2 * RANGE + 1
OFFSETS = (-2, -1, 1, 2)
RETURNS = (2, 1, -1, -2)

EPS = 1e-06
ROOT_HALF = 0.7071067811865476
INV_ROOT_TAU = 0.3989422804014327

TS = 16
CELLS = TS * TS
C = 128
F = 512
FC = 256
SLOTS = 2
RIM = 160
RING_S = 320
RING_T = 272
BLOCK = 64
TILE_ROWS = 4 * BLOCK
BINS = WINDOW * SLOTS * TILE_ROWS + BLOCK
AT_CELL, AT_RIM, AT_PUT, AT_TAKE, AT_OUT, AT_END = 0, 256, 512, 832, 1104, 1264
GROWS = 1152
SMALL = 1024
VMEM = 14 * 1024 * 1024

f32 = jnp.float32
bf16 = jnp.bfloat16


def rim_of_cell():
    rim = np.full((TS, TS), -1, np.int32)
    for i in range(TS):
        for j in range(TS):
            if i < 3:
                rim[i, j] = i * TS + j
            elif i >= 13:
                rim[i, j] = 48 + (i - 13) * TS + j
            elif j < 3:
                rim[i, j] = 96 + (i - 3) * 6 + j
            elif j >= 13:
                rim[i, j] = 96 + (i - 3) * 6 + 3 + (j - 13)
    return rim


def pieces_of(code):
    turned = np.rot90(np.arange(CELLS).reshape(TS, TS), code)
    out = np.full((BLOCK,), -1, np.int32)
    out[0:48] = turned[0:3][::-1, ::-1].reshape(-1)
    out[48:57] = turned[0:3, 0:3][::-1, ::-1].reshape(-1)
    return out


def frame_positions():
    frame = np.arange(22 * 22).reshape(22, 22)
    row = np.full((22 * 22,), -1, np.int32)
    for q in range(4):
        turned = np.rot90(frame, q)
        row[turned[0:3, 3:19].reshape(-1)] = q * 48 + np.arange(48)
        row[turned[0:3, 0:3].reshape(-1)] = 192 + q * 16 + np.arange(9)
    return row.reshape(22, 22)


def order_s():
    out = []
    for rows in (range(0, 3), range(19, 22)):
        for p in rows:
            out += [(p, cc - 5) if 0 <= cc - 5 < 22 else None for cc in range(32)]
    for p in range(3, 19):
        out += [(p, 19), (p, 20), (p, 21), None, None, (p, 0), (p, 1), (p, 2)]
    return out


def order_t():
    out = []
    for rows in (range(0, 3), range(19, 22)):
        for p in rows:
            out += [(p, cc) if cc < 22 else None for cc in range(24)]
    for p in range(3, 19):
        out += [(p, 0), (p, 1), (p, 2), (p, 19), (p, 20), (p, 21), None, None]
    return out


def fixed_rows():
    rim = rim_of_cell().reshape(-1)
    cell_of_rim = np.full((RIM,), -1, np.int32)
    for cell in range(CELLS):
        if rim[cell] >= 0:
            cell_of_rim[rim[cell]] = cell
    codes = np.concatenate([pieces_of(code) for code in range(4)])
    from_rim = np.where(codes >= 0, rim[codes], -1)
    at = frame_positions()
    put = np.array([-1 if p is None else at[p] for p in order_s()], np.int32)
    take = np.array([-1 if p is None else at[p] for p in order_t()], np.int32)
    return np.concatenate([codes, from_rim, put, take, cell_of_rim]).astype(np.int32)


def dot(a, b):
    return lax.dot_general(a, b, (((1,), (0,)), ((), ())), preferred_element_type=f32)


def dot_nt(a, b):
    return lax.dot_general(a, b, (((1,), (1,)), ((), ())), preferred_element_type=f32)


def dot_tn(a, b):
    return lax.dot_general(a, b, (((0,), (0,)), ((), ())), preferred_element_type=f32)


def assemble(pad_ref, t, ring, center):
    pad_ref[t, 0:3] = ring[0:96].reshape(3, 32, C)
    pad_ref[t, 19:22] = ring[96:192].reshape(3, 32, C)
    sides = ring[192:320].reshape(TS, 8, C)
    pad_ref[t, 3:19, 0:8] = sides
    pad_ref[t, 3:19, 24:32] = sides
    pad_ref[t, 3:19, 8:24] = center.astype(f32).reshape(TS, TS, C)


def depthwise(pad_ref, k_ref, b, bias, conv_ref):
    for t in range(SLOTS):
        for half in range(2):
            total = jnp.broadcast_to(bias.reshape(1, 1, C), (8, TS, C))
            for e in range(7):
                moved = pad_ref[t, 8 * half : 8 * half + 14, 5 + e : 21 + e, :]
                for a in range(7):
                    tap = k_ref[b, 7 * a + e : 7 * a + e + 1, :].reshape(1, 1, C)
                    total = total + tap * moved[a : a + 8]
            at = t * CELLS + half * 128
            conv_ref[at : at + 128] = total.reshape(128, C)


def normalise(conv, gain, shift):
    centred = conv - jnp.mean(conv, axis=-1, keepdims=True)
    inverse = lax.rsqrt(jnp.mean(centred * centred, axis=-1, keepdims=True) + EPS)
    unit = centred * inverse
    return unit, inverse, (unit * gain + shift).astype(bf16)


def spread(g_conv, gc_ref, k_ref, b, g_ref):
    for t in range(SLOTS):
        gc_ref[t, :, 0:8] = jnp.zeros((TS, 8, C), f32)
        gc_ref[t, :, 24:32] = jnp.zeros((TS, 8, C), f32)
        gc_ref[t, :, 8:24] = g_conv[t * CELLS : (t + 1) * CELLS].reshape(TS, TS, C)
    for t in range(SLOTS):
        for first, last in ((0, 6), (6, 11), (11, 16), (16, 22)):
            totals = [None] * (last - first)
            low, high = max(0, first - 6), min(TS, last)
            for e in range(7):
                moved = gc_ref[t, low:high, 8 - e : 32 - e, :]
                for a in range(7):
                    tap = k_ref[b, 7 * a + e : 7 * a + e + 1, :]
                    for p in range(first, last):
                        r = p - a
                        if 0 <= r < TS:
                            term = tap * moved[r - low]
                            was = totals[p - first]
                            totals[p - first] = term if was is None else was + term
            for p in range(first, last):
                g_ref[t, p] = totals[p - first]


def ring_out(g_ref, ring_ref):
    for t in range(SLOTS):
        at = t * RING_T
        ring_ref[at : at + 72] = g_ref[t, 0:3].reshape(72, C).astype(bf16)
        ring_ref[at + 72 : at + 144] = g_ref[t, 19:22].reshape(72, C).astype(bf16)
        left = g_ref[t, 3:19, 0:8]
        right = g_ref[t, 3:19, 16:24]
        column = lax.broadcasted_iota(jnp.int32, (TS, 8, C), 1)
        ring_ref[at + 144 : at + 272] = jnp.where(column < 3, left, right).reshape(128, C).astype(bf16)


def kernel_terms(pad_ref, gc_ref, grads_ref):
    for e in range(7):
        sums = [None] * 7
        for t in range(SLOTS):
            for half in range(2):
                moved = pad_ref[t, 8 * half : 8 * half + 14, 5 + e : 21 + e, :]
                here = gc_ref[t, 8 * half : 8 * half + 8, 8:24]
                for a in range(7):
                    part = jnp.sum(here * moved[a : a + 8], axis=0)
                    part = part[0:8] + part[8:16]
                    sums[a] = part if sums[a] is None else sums[a] + part
        for a in range(7):
            at = SMALL + 7 * a + e
            grads_ref[at : at + 1] = jnp.sum(sums[a], axis=0, keepdims=True)


def column_sum(x):
    return jnp.sum(x, axis=0, keepdims=True)


def bias_in(small_ref, b, at):
    first = 4 + at // C
    return jnp.concatenate([small_ref[b, r : r + 1] for r in range(first, first + FC // C)], axis=1)


def pointwise_back(b, unit, inverse, normed, g_branch, wts, kept):
    small_ref, w_in_ref, w_out_ref = wts
    act_ref, g_pre_ref, g_bias_ref, g_normed_ref = kept
    g_normed = None
    for at in range(0, F, FC):
        w1 = w_in_ref[b, 0:C, at : at + FC]
        w2 = w_out_ref[b, at : at + FC, :]
        pre = dot(normed, w1) + bias_in(small_ref, b, at)
        half = 0.5 * (1.0 + lax.erf(pre * ROOT_HALF))
        act_ref[:, at : at + FC] = (pre * half).astype(bf16)
        slope = half + pre * INV_ROOT_TAU * jnp.exp(-0.5 * pre * pre)
        g_pre = dot_nt(g_branch, w2) * slope
        g_bias_ref[0:1, at : at + FC] = column_sum(g_pre)
        g_pre_b = g_pre.astype(bf16)
        g_pre_ref[:, at : at + FC] = g_pre_b
        part = dot_nt(g_pre_b, w1)
        g_normed = part if g_normed is None else g_normed + part
    g_normed_ref[...] = g_normed
    g_unit = g_normed * small_ref[b, 1:2]
    return inverse * (
        g_unit
        - jnp.mean(g_unit, axis=-1, keepdims=True)
        - unit * jnp.mean(g_unit * unit, axis=-1, keepdims=True)
    )


def weight_terms(pad_ref, gc_ref, unit, normed, g_branch, kept, grads_ref):
    act_ref, g_pre_ref, g_bias_ref, g_normed_ref = kept
    grads_ref[SMALL + 49 : GROWS] = jnp.zeros((GROWS - SMALL - 49, C), f32)
    for at in range(0, F, FC):
        g_w1 = dot_tn(normed, g_pre_ref[:, at : at + FC])
        for c0 in range(0, FC, C):
            grads_ref[at + c0 : at + c0 + C] = g_w1[:, c0 : c0 + C]
            row = SMALL + 52 + (at + c0) // C
            grads_ref[row : row + 1] = g_bias_ref[0:1, at + c0 : at + c0 + C]
        grads_ref[512 + at : 512 + at + FC] = dot_tn(act_ref[:, at : at + FC], g_branch)
    g_normed = g_normed_ref[...]
    g_conv_sum = sum(jnp.sum(gc_ref[t, :, 8:24].reshape(CELLS, C), axis=0, keepdims=True) for t in range(SLOTS))
    grads_ref[SMALL + 49 : SMALL + 50] = g_conv_sum
    grads_ref[SMALL + 50 : SMALL + 51] = column_sum(g_normed * unit)
    grads_ref[SMALL + 51 : SMALL + 52] = column_sum(g_normed)
    grads_ref[SMALL + 56 : SMALL + 57] = column_sum(g_branch.astype(f32))
    kernel_terms(pad_ref, gc_ref, grads_ref)


def picked(start, canon, t):
    parts = []
    for q in range(8):
        first = pl.multiple_of(start[t, q], BLOCK)
        parts.append(canon[pl.ds(first, 48), :] if q < 4 else canon[pl.ds(first + 48, 16), :])
    return jnp.concatenate(parts, axis=0)


def put_pieces(start, fixed, ring_ref, bins, piece_refs):
    bins[...] = jnp.zeros((BINS, C), f32)
    for t in range(SLOTS):
        ring = ring_ref[t * RING_T : (t + 1) * RING_T]
        parts = dot_tn(fixed[AT_TAKE:AT_OUT, :], ring)
        for q in range(8):
            first = pl.multiple_of(start[t, q], BLOCK)
            if q < 4:
                bins[pl.ds(first, 48), :] += parts[q * 48 : (q + 1) * 48]
            else:
                bins[pl.ds(first + 48, 16), :] += parts[192 + (q - 4) * 16 : 208 + (q - 4) * 16]
    to_rim = fixed[AT_RIM:AT_PUT, 0:RIM]
    for o in range(WINDOW):
        for t in range(SLOTS):
            at = (o * SLOTS + t) * TILE_ROWS
            given = bins[at : at + TILE_ROWS].astype(bf16)
            piece_refs[o][t * RIM : (t + 1) * RIM] = dot_tn(to_rim, given).astype(bf16)


def put_base(g_ref, upstream, base_ref):
    for t in range(SLOTS):
        center = g_ref[t, 3:19, 3:19, :].reshape(CELLS, C).astype(bf16).astype(f32)
        base_ref[t] = upstream[t * CELLS : (t + 1) * CELLS] + center


def combined(base_ref, pieces, fixed):
    to_cell = fixed[AT_OUT:AT_END, :]
    out = []
    for t in range(SLOTS):
        total = sum(p[t * RIM : (t + 1) * RIM].astype(f32) for p in pieces)
        high = total.astype(bf16)
        low = (total - high.astype(f32)).astype(bf16)
        out.append((base_ref[t] + (dot_tn(to_cell, high) + dot_tn(to_cell, low))).astype(bf16))
    return out


def first_kernel(start, own, m2, m1, p1, p2, fixed, mask, k, small, w_in, w_out,
                 out, rims, pad_b, conv, canon, pad):
    canon[BINS - BLOCK :] = jnp.zeros((BLOCK, C), bf16)
    for o, ref in enumerate((m2, m1, own, p1, p2)):
        for t in range(SLOTS):
            at = (o * SLOTS + t) * TILE_ROWS
            canon[at : at + TILE_ROWS] = dot(fixed[AT_CELL:AT_RIM, :], ref[t, 0:CELLS]).astype(bf16)
    for t in range(SLOTS):
        assemble(pad, t, dot(fixed[AT_PUT:AT_TAKE, :], picked(start, canon, t)), own[t, 0:CELLS])
    pad_b[...] = pad[...].astype(bf16)
    depthwise(pad, k, 0, small[0, 0:1], conv)
    unit, inverse, normed = normalise(conv[...], small[0, 1:2], small[0, 2:3])
    branch = None
    for at in range(0, F, FC):
        pre = dot(normed, w_in[0, 0:C, at : at + FC]) + bias_in(small, 0, at)
        act = (0.5 * pre * (1.0 + lax.erf(pre * ROOT_HALF))).astype(bf16)
        part = dot(act, w_out[0, at : at + FC, :])
        branch = part if branch is None else branch + part
    branch = branch + small[0, 3:4]
    for t in range(SLOTS):
        lo, hi = t * CELLS, (t + 1) * CELLS
        value = (own[t, 0:CELLS].astype(f32) + mask[lo:hi] * branch[lo:hi]).astype(bf16)
        out[t] = value
        rims[t * RIM : (t + 1) * RIM] = dot(fixed[AT_OUT:AT_END, :], value).astype(bf16)


def middle_kernel(start, own, r_own, m2, m1, p1, p2, fixed, cot, mask, k, small, w_in, w_out,
                  q0, q1, q2, q3, q4, base, pad, gc, unit_out, normed_out, g_branch_out, act, g_pre, g_bias, g_normed,
                  canon, conv, g, ring_b, bins):
    canon[BINS - BLOCK :] = jnp.zeros((BLOCK, C), bf16)
    for o, ref in enumerate((m2, m1, r_own, p1, p2)):
        for t in range(SLOTS):
            at = (o * SLOTS + t) * TILE_ROWS
            tile = ref[t * RIM : (t + 1) * RIM]
            canon[at : at + TILE_ROWS] = dot(fixed[AT_RIM:AT_PUT, 0:RIM], tile).astype(bf16)
    for t in range(SLOTS):
        assemble(pad, t, dot(fixed[AT_PUT:AT_TAKE, :], picked(start, canon, t)), own[t])
    depthwise(pad, k, 1, small[1, 0:1], conv)
    unit, inverse, normed = normalise(conv[...], small[1, 1:2], small[1, 2:3])
    upstream = cot[...].reshape(SLOTS * CELLS, C)
    g_branch = upstream * mask[...].astype(bf16)
    unit_out[...] = unit
    normed_out[...] = normed
    g_branch_out[...] = g_branch
    g_conv = pointwise_back(
        1, unit, inverse, normed, g_branch, (small, w_in, w_out), (act, g_pre, g_bias, g_normed)
    )
    spread(g_conv, gc, k, 1, g)
    ring_out(g, ring_b)
    put_pieces(start, fixed, ring_b, bins, (q0, q1, q2, q3, q4))
    put_base(g, upstream.astype(f32), base)


def middle_rest_kernel(own, pad, gc, unit, normed, g_branch, act, g_pre, g_bias, g_normed, mask, small, w_out,
                       out, grads):
    branch = dot(act[...], w_out[1, 0:F]) + small[1, 3:4]
    for t in range(SLOTS):
        lo, hi = t * CELLS, (t + 1) * CELLS
        out[t] = (own[t].astype(f32) + mask[lo:hi] * branch[lo:hi]).astype(bf16)
    weight_terms(pad, gc, unit[...], normed[...], g_branch[...], (act, g_pre, g_bias, g_normed), grads)


def last_kernel(start, base_in, i0, i1, i2, i3, i4, fixed, conv, mask, k, small, w_in, w_out,
                q0, q1, q2, q3, q4, base, gc, unit_out, normed_out, g_branch_out, act, g_pre, g_bias, g_normed,
                g, ring_b, bins):
    parts = combined(base_in, [r[...] for r in (i0, i1, i2, i3, i4)], fixed)
    upstream = jnp.concatenate(parts, axis=0)
    g_branch = upstream * mask[...].astype(bf16)
    unit, inverse, normed = normalise(conv[...], small[0, 1:2], small[0, 2:3])
    unit_out[...] = unit
    normed_out[...] = normed
    g_branch_out[...] = g_branch
    g_conv = pointwise_back(
        0, unit, inverse, normed, g_branch, (small, w_in, w_out), (act, g_pre, g_bias, g_normed)
    )
    spread(g_conv, gc, k, 0, g)
    ring_out(g, ring_b)
    put_pieces(start, fixed, ring_b, bins, (q0, q1, q2, q3, q4))
    put_base(g, upstream.astype(f32), base)


def last_rest_kernel(pad_b, gc, unit, normed, g_branch, act, g_pre, g_bias, g_normed, grads1, packed, pad):
    pad[...] = pad_b[...].astype(f32)
    packed[GROWS:] = grads1[...]
    weight_terms(pad, gc, unit[...], normed[...], g_branch[...], (act, g_pre, g_bias, g_normed), packed)


def closing_kernel(base_in, i0, i1, i2, i3, i4, fixed, out):
    parts = combined(base_in, [r[...] for r in (i0, i1, i2, i3, i4)], fixed)
    for t in range(SLOTS):
        out[t] = parts[t]


def unpack_kernel(scale, packed, dw, dwb, gain, shift, w_in, b_in, w_out, b_out):
    for b in range(BLOCKS):
        at = b * GROWS
        value = packed[at : at + GROWS].astype(f32) * scale
        for c0 in range(0, F, C):
            w_in[b, :, c0 : c0 + C] = value[c0 : c0 + C]
            row = SMALL + 52 + c0 // C
            b_in[b : b + 1, c0 : c0 + C] = value[row : row + 1]
        w_out[b] = value[512:1024]
        dw[:, b, :] = value[SMALL : SMALL + 49]
        dwb[b : b + 1] = value[SMALL + 49 : SMALL + 50]
        gain[b : b + 1] = value[SMALL + 50 : SMALL + 51]
        shift[b : b + 1] = value[SMALL + 51 : SMALL + 52]
        b_out[b : b + 1] = value[SMALL + 56 : SMALL + 57]


def shape(dims, kind):
    return jax.ShapeDtypeStruct(dims, kind)


def call(kernel, outs, args, scratch=(), scalars=0, flops=1000000, name=None):
    vmem = pl.BlockSpec(memory_space=pltpu.VMEM)
    size = sum(math.prod(a.shape) * a.dtype.itemsize for a in list(args) + list(outs))
    return pl.pallas_call(
        kernel,
        out_shape=outs,
        in_specs=[pl.BlockSpec(memory_space=pltpu.SMEM)] * scalars + [vmem] * (len(args) - scalars),
        out_specs=[vmem] * len(outs),
        scratch_shapes=list(scratch),
        compiler_params=pltpu.CompilerParams(vmem_limit_bytes=VMEM),
        cost_estimate=pl.CostEstimate(flops=flops, bytes_accessed=size, transcendentals=0),
        name=name,
    )(*args)


def shift_by(x, by):
    n = lax.axis_size("space")
    return lax.ppermute(x, "space", [(i, (i + by) % n) for i in range(n)])


def strides(axis):
    return {"core": (1, 2), "z": (2, 4), "x": (8, 4), "y": (32, 4)}[axis]


def coordinate(axis):
    stride, extent = strides(axis)
    return (lax.axis_index("space") // stride) % extent


def along(x, axis, move):
    stride, extent = strides(axis)
    pairs = []
    for i in range(lax.axis_size("space")):
        c = (i // stride) % extent
        pairs.append((i, i + (move(c) - c) * stride))
    return lax.ppermute(x, "space", pairs)


def scatter_sum(x, axis, kind):
    extent = strides(axis)[1]
    me = coordinate(axis)
    parts = x.reshape((extent, -1, C))
    total = lax.dynamic_index_in_dim(parts, me, 0, keepdims=False)
    for d in range(1, extent):
        piece = lax.dynamic_index_in_dim(parts, (me + d) % extent, 0, keepdims=False).astype(kind)
        total = total + along(piece, axis, lambda c: (c + d) % extent).astype(f32)
    return total


def exchange_sum(x, axis, mask):
    return x + along(x, axis, lambda c: c ^ mask)


def collect(x, axis):
    extent = strides(axis)[1]
    me = coordinate(axis)
    out = lax.dynamic_update_index_in_dim(jnp.zeros((extent,) + x.shape, x.dtype), x, me, 0)
    for d in range(1, extent):
        got = along(x, axis, lambda c: (c + d) % extent)
        out = lax.dynamic_update_index_in_dim(out, got, (me - d) % extent, 0)
    return out.reshape(-1, C)


def pair_sum(x):
    n = lax.axis_size("space")
    stride, extent = strides("z")

    def other(flip, mask):
        pairs = []
        for i in range(2 * n):
            half, s = i // n, i % n
            z = (s // stride) % extent
            pairs.append((i, (half ^ flip) * n + s + ((z ^ mask) - z) * stride))
        return lax.ppermute(x, ("dp", "space"), pairs)

    got = [other(1, 0), other(1, 2), other(0, 2)]
    return (x + got[2]) + (got[0] + got[1])


def reduced(g, beside):
    x = scatter_sum(g, "core", f32)
    x, *beside = lax.optimization_barrier((x, *beside))
    x = scatter_sum(x, "x", bf16)
    x = scatter_sum(x, "y", bf16)
    x = exchange_sum(x, "z", 1)
    x = pair_sum(x)
    x = x.astype(bf16)
    x = collect(x, "y")
    x = collect(x, "x")
    return collect(x, "core"), beside


def piece_starts(neighbors, codes):
    n = lax.axis_size("space")
    distance = jnp.mod(jnp.floor_divide(neighbors, SLOTS) - lax.axis_index("space"), n)
    distance = jnp.where(distance > n // 2, distance - n, distance)
    begin = ((distance + RANGE) * SLOTS + jnp.mod(neighbors, SLOTS)) * TILE_ROWS + codes * BLOCK
    return jnp.where(neighbors >= 0, begin, BINS - BLOCK).astype(jnp.int32)


def local(fields, cotangent, ocean_mask, neighbors, codes, dw_kernel, dw_bias, ln_gain, ln_bias, w_in, b_in, w_out,
          b_out):
    dims = fields.shape
    own = fields.reshape(SLOTS, CELLS, C)
    raw = [shift_by(own, -o) for o in OFFSETS]
    start = piece_starts(neighbors, codes)
    fixed = (jnp.asarray(fixed_rows())[:, None] == jnp.arange(CELLS, dtype=jnp.int32)[None, :]).astype(bf16)
    mask = ocean_mask.astype(f32).reshape(SLOTS * CELLS, 1)
    rows = [p.reshape(BLOCKS, 1, C) for p in (dw_bias, ln_gain, ln_bias, b_out)]
    small = jnp.concatenate(rows + [b_in.reshape(BLOCKS, F // C, C)], axis=1)
    w_in = jnp.pad(w_in, ((0, 0), (0, 16), (0, 0)))
    w_out = jnp.pad(w_out, ((0, 0), (0, 16), (0, 0)))
    center = jnp.pad(own, ((0, 0), (0, 16), (0, 0)))
    start, fixed, mask, small, w_in, w_out, center = lax.optimization_barrier(
        (start, fixed, mask, small, w_in, w_out, center)
    )
    tile = (SLOTS, CELLS, C)
    flat = (SLOTS * CELLS, C)
    wide = (SLOTS * CELLS, F)
    padded = (SLOTS, 22, 32, C)
    rims_shape = shape((SLOTS * RIM, C), bf16)
    out0, rims, pad0, conv0 = call(
        first_kernel,
        [shape(tile, bf16), rims_shape, shape(padded, bf16), shape(flat, f32)],
        [start, center, *raw, fixed, mask, dw_kernel, small, w_in, w_out],
        [pltpu.VMEM((BINS, C), bf16), pltpu.VMEM(padded, f32)],
        scalars=1, flops=2000000000, name="block0_forward",
    )
    got = [shift_by(rims, -o) for o in OFFSETS]
    back = [
        pltpu.VMEM((SLOTS, 22, 24, C), f32), pltpu.VMEM((SLOTS * RING_T, C), bf16), pltpu.VMEM((BINS, C), f32)
    ]
    kept = [
        shape((SLOTS, TS, 32, C), f32), shape(flat, f32), shape(flat, bf16), shape(flat, bf16),
        shape(wide, bf16), shape(wide, bf16), shape((1, F), f32), shape(flat, f32),
    ]
    q0, q1, q2, q3, q4, base1, pad1, *saved = call(
        middle_kernel,
        [rims_shape] * 5 + [shape(tile, f32), shape(padded, f32)] + kept,
        [start, out0, rims, *got, fixed, cotangent.reshape(tile), mask, dw_kernel, small, w_in, w_out],
        [pltpu.VMEM((BINS, C), bf16), pltpu.VMEM(flat, f32)] + back,
        scalars=1, flops=4000000000, name="block1_both",
    )
    pieces = [q2] + [shift_by(q, o) for q, o in zip((q4, q3, q1, q0), RETURNS)]
    out1, grads1 = call(
        middle_rest_kernel,
        [shape(tile, bf16), shape((GROWS, C), f32)],
        [out0, pad1, *saved, mask, small, w_out],
        flops=4000000000, name="block1_rest",
    )
    q0, q1, q2, q3, q4, base0, *saved = call(
        last_kernel,
        [rims_shape] * 5 + [shape(tile, f32)] + kept,
        [start, base1, *pieces, fixed, conv0, mask, dw_kernel, small, w_in, w_out],
        back,
        scalars=1, flops=3000000000, name="block0_backward",
    )
    pieces = [q2] + [shift_by(q, o) for q, o in zip((q4, q3, q1, q0), RETURNS)]
    (packed,) = call(
        last_rest_kernel,
        [shape((BLOCKS * GROWS, C), f32)],
        [pad0, *saved, grads1],
        [pltpu.VMEM(padded, f32)],
        flops=4000000000, name="block0_rest",
    )
    packed, pieces = reduced(packed, pieces)
    (field_grad,) = call(
        closing_kernel, [shape(tile, bf16)], [base0, *pieces, fixed], flops=100000000, name="closing"
    )
    scale = 1.0 / math.sqrt(SLOTS * CELLS * lax.axis_size("dp") * lax.axis_size("space"))
    grads = call(
        lambda *refs: unpack_kernel(scale, *refs),
        [
            shape((49, BLOCKS, C), f32), shape((BLOCKS, C), f32), shape((BLOCKS, C), f32), shape((BLOCKS, C), f32),
            shape((BLOCKS, C, F), f32), shape((BLOCKS, F), f32), shape((BLOCKS, F, C), f32), shape((BLOCKS, C), f32),
        ],
        [packed], flops=1000000, name="unpack",
    )
    return (out1.reshape(dims), field_grad.reshape(dims), jnp.transpose(grads[0], (1, 0, 2)), *grads[1:])


def solution(mesh):
    placed = (
        P("dp", "space", None, None, None),
        P("dp", "space", None, None, None),
        P("space", None, None),
        P("space", None),
        P("space", None),
    ) + (P(),) * 8
    return jax.shard_map(
        local,
        mesh=mesh,
        in_specs=placed,
        out_specs=(P("dp", "space", None, None, None), P("dp", "space", None, None, None)) + (P(),) * 8,
        check_vma=False,
    )
```
